32 devices in a mesh: role: 2 (over core), dev: 8 (over z, y), head: 2 (over x).
Axes of the slice: x: 2, y: 2, z: 4, core: 2. Of those that a mesh axis runs over, the one named last changes fastest.
Arguments:
- hidden: bfloat16 [256, 4096], P(('role', 'dev', 'head')), may hold values from -6 to 6
- queries: bfloat16 [256, 64, 128], P(('role', 'dev'), 'head'), as said below
- cache_keys: bfloat16 [256, 128, 4, 128], P(('role', 'dev'), None, 'head'), as said below
- cache_values: bfloat16 [256, 128, 4, 128], P(('role', 'dev'), None, 'head'), may hold values from -6 to 6
- new_keys: bfloat16 [256, 4, 128], P(('role', 'dev'), 'head'), may hold values from -6 to 6
- new_values: bfloat16 [256, 4, 128], P(('role', 'dev'), 'head'), may hold values from -6 to 6
- lengths: int32 [256], P(('role', 'dev')), may hold values from 32 to 128, as said below
- out_proj: bfloat16 [8192, 4096], P('head', 'dev'), may hold values from -0.5 to 0.5
- norm_gain: float32 [4096], replicated, may hold values from 0.1 to 1.9
- expert_gate: bfloat16 [16, 4096, 768], P(('role', 'dev'), None, 'head'), may hold values from -0.09375 to 0.09375
- expert_up: bfloat16 [16, 4096, 768], P(('role', 'dev'), None, 'head'), may hold values from -0.09375 to 0.09375
- expert_down: bfloat16 [16, 768, 4096], P(('role', 'dev'), 'head'), may hold values from -0.21875 to 0.21875
- expert_ids: int32 [256, 8], P(('role', 'dev', 'head')), may hold values from 0 to 15, all different within a row; in each aligned block of 8 rows (0 to 7, 8 to 15, ...) at most 8 rows name the same one
- gate_levels: int32 [256, 8], P(('role', 'dev', 'head')), may hold values from 1 to 255
Outputs:
- layer_out: bfloat16 [256, 4096], P(('role', 'dev', 'head'))
The draws below stay inside these ranges and needn't reach their ends.
Inputs may be any that keep to these rules, and one draw needn't show every extreme that they name: `queries`: query vectors of the new tokens. `cache_keys`: cached keys of the requests. `lengths`: the first request of each block of 16 rows holds 128 positions and the second holds 32. `expert_ids`: each row names 8 different experts; among the 8 rows of one device no expert is named more than 8 times, a bound that some block reaches.
All inputs are finite; a program needn't handle non-finite values.
Results may differ from the reference program's by a relative error of at most 0.0065.
Values may be sent and summed in bfloat16 or wider, within the bound.
A program may use at most 64 MiB of HBM per device.

```python
import math
import jax
import jax.numpy as jnp
import numpy as np
from jax import lax

D = 4096
QH = 64
KVH = 4
HD = 128
TOPK = 8
FF = 768
CACHE = 128
R_DEV = 16
TOK_DEV = 8
ROWS = 256
EXPERTS = 16
CAP = 8


def key_field(key):
    sampled = jax.random.normal(jax.random.fold_in(key, 31), (ROWS, CACHE, KVH, HD), jnp.float32)
    return sampled


def draw_cache_keys(key, part):
    return key_field(key).astype(jnp.bfloat16)


def draw_queries(key, part):
    sampled = jax.random.normal(jax.random.fold_in(key, 32), (ROWS, QH, HD), jnp.float32)
    return sampled.astype(jnp.bfloat16)


def draw_lengths(key, part):
    drawn = jax.random.randint(jax.random.fold_in(key, 41), (ROWS,), CACHE // 4, CACHE + 1, jnp.int32)
    position = jnp.arange(ROWS, dtype=jnp.int32) % R_DEV
    drawn = jnp.where(position == 0, CACHE, drawn)
    drawn = jnp.where(position == 1, CACHE // 4, drawn)
    return drawn.astype(jnp.int32)


def with_ends(values, rng, low, high):
    place = [jax.random.randint(jax.random.fold_in(rng, axis), (), 0, length) for axis, length in enumerate(values.shape)]
    longest = values.shape.index(max(values.shape))
    beside = place[:longest] + [(place[longest] + 1) % values.shape[longest]] + place[longest + 1:]
    return values.at[tuple(place)].set(low).at[tuple(beside)].set(high)


def steps_of(key, extent, shards, smallest, high):
    level, own = 1.0, jax.random.fold_in(key, 6)
    for axis_at, shards_of in shards:
        steps = jnp.exp(jax.random.uniform(jax.random.fold_in(own, axis_at), (shards_of,), jnp.float32, smallest / len(shards), high / len(shards)))
        level = level * jnp.repeat(steps, extent[axis_at] // shards_of).reshape([-1 if axis == axis_at else 1 for axis in range(len(extent))])
    return level


def shared_out(rng, own, number, rows, count, top, most, skew):
    order = jax.random.permutation(rng, count)
    heavy_load, usual = load_shares(count, rows * top, most, skew, True), load_shares(count, rows * top, most, skew, False)
    places = jnp.arange(count)

    def named(sizes, turn):
        used = int((sizes > 0).sum())
        fixed = max(1, used // 4)
        passed = fixed + (places - fixed + turn * (used - fixed)) % max(1, count - fixed)
        return jnp.zeros((count,), jnp.int32).at[order[jnp.where(places < fixed, places, passed)]].set(jnp.asarray(sizes, jnp.int32))

    sizes = jnp.where(number % 4 == 0, named(heavy_load, number // 4), named(usual, number - number // 4 - 1))
    mixed = jax.random.permutation(jax.random.fold_in(own, 3), count)
    giver, receiver = mixed[0:count // 2 * 2:2], mixed[1:count // 2 * 2:2]
    slack = jnp.minimum(sizes[giver] - 1, most - sizes[receiver]) // 2
    slack = jnp.where((giver == order[0]) | (receiver == order[0]) | (sizes[receiver] == 0), 0, jnp.maximum(slack, 0))
    passed = jax.random.randint(jax.random.fold_in(own, 4), (count // 2,), 0, 1 << 20) % (slack + 1)
    sizes = sizes.at[giver].add(-passed).at[receiver].add(passed)
    items = jnp.searchsorted(jnp.cumsum(sizes), jnp.arange(rows * top), side="right").astype(jnp.int32)
    table = items.reshape(top, rows).T
    table = table[jax.random.permutation(jax.random.fold_in(own, 1), rows)]
    turn = jax.random.randint(jax.random.fold_in(own, 2), (rows, 1), 0, top)
    return jnp.take_along_axis(table, (jnp.arange(top)[None, :] + turn) % top, axis=1)


def load_shares(amount, total, bound, skew, full):
    weights = [(1 << 20) // math.isqrt(rank ** skew) + 1 for rank in range(1, amount + 1)]
    largest = bound if full else min(bound, max(-(-total // amount), total * weights[0] // sum(weights)))
    least = 1 if total - largest >= amount - 1 else 0
    counts, spare = [largest] + [least] * (amount - 1), total - largest - least * (amount - 1)
    while spare > 0:
        movable = [i for i in range(1, amount) if counts[i] < largest] or [i for i in range(1, amount) if counts[i] < bound]
        whole, remaining = sum([weights[i] for i in movable]), spare
        for i in movable:
            addition = min(bound - counts[i], max(1, remaining * weights[i] // whole), spare)
            counts[i] = counts[i] + addition
            spare = spare - addition
    return np.array(counts)


def normal_values(stream_key, extent, scale, bound, shards=(), held_as=jnp.bfloat16):
    gain = steps_of(stream_key, extent, shards, -0.22, 0.18) if shards else 1.0
    result = jax.random.normal(stream_key, extent, jnp.float32) * scale * gain
    return jnp.minimum(jnp.maximum(result, -bound), bound).astype(held_as)


def setup_inputs(seed: int = 0) -> dict:
    key_list = jax.random.split(jax.random.key(seed), 15)
    hidden = normal_values(key_list[0], (ROWS, D), 1.0, 6.0, ((0, 32),))
    queries = draw_queries(jax.random.fold_in(key_list[14], 71), 0)
    cache_keys = draw_cache_keys(jax.random.fold_in(key_list[14], 71), 0)
    cache_values = normal_values(key_list[3], (ROWS, CACHE, KVH, HD), 1.0, 6.0, ((0, 16), (2, 2)))
    new_keys = normal_values(key_list[4], (ROWS, KVH, HD), 1.0, 6.0, ((0, 16), (1, 2)))
    new_values = normal_values(key_list[5], (ROWS, KVH, HD), 1.0, 6.0, ((0, 16), (1, 2)))
    lengths = draw_lengths(jax.random.fold_in(key_list[14], 71), 0)
    out_proj = normal_values(key_list[7], (QH * HD, D), HD ** -0.5, 0.5, ((0, 2), (1, 8)))
    norm_gain = jnp.clip(1.0 + 0.18 * jax.random.normal(key_list[8], (D,), jnp.float32), 0.1, 1.9)
    expert_gate = normal_values(key_list[9], (EXPERTS, D, FF), D ** -0.5, 0.09375, ((0, 16), (2, 2)))
    expert_up = normal_values(key_list[10], (EXPERTS, D, FF), D ** -0.5, 0.09375, ((0, 16), (2, 2)))
    expert_down = normal_values(key_list[11], (EXPERTS, FF, D), FF ** -0.5, 0.21875, ((0, 16), (1, 2)))
    expert_ids_keys = jax.random.split(jax.random.fold_in(key_list[12], 1), ROWS // TOK_DEV)
    expert_ids_turns = jax.random.permutation(jax.random.fold_in(key_list[12], 3), ROWS // TOK_DEV)
    expert_ids = jax.vmap(lambda own, number: shared_out(jax.random.fold_in(key_list[12], 2), own, number, TOK_DEV, EXPERTS, TOPK, CAP, 2))(expert_ids_keys, expert_ids_turns).reshape((ROWS, TOPK))
    gate_levels = with_ends(jax.random.randint(key_list[13], (ROWS, TOPK), 1, 256), jax.random.fold_in(key_list[13], 1), 1, 255).astype(jnp.int32)
    return dict(hidden=hidden, queries=queries, cache_keys=cache_keys, cache_values=cache_values, new_keys=new_keys, new_values=new_values, lengths=lengths, out_proj=out_proj, norm_gain=norm_gain, expert_gate=expert_gate, expert_up=expert_up, expert_down=expert_down, expert_ids=expert_ids, gate_levels=gate_levels)


def attend_block(query_rows, key_rows, value_rows, key_new, value_new, valid_len):
    row_count = query_rows.shape[0]
    kv_heads = key_rows.shape[2]
    group_size = query_rows.shape[1] // kv_heads
    head_dim = query_rows.shape[2]
    scaling = 1.0 / math.sqrt(head_dim)
    query_f = query_rows.astype(jnp.float32).reshape(row_count, kv_heads, group_size, head_dim)
    scores = jnp.einsum('bhgd,bthd->bhgt', query_f, key_rows.astype(jnp.float32)) * scaling
    scores_new = jnp.einsum('bhgd,bhd->bhg', query_f, key_new.astype(jnp.float32)) * scaling
    positions = jnp.arange(key_rows.shape[1], dtype=jnp.int32)
    usable = (positions[None, :] < valid_len[:, None])[:, None, None, :]
    masked = jnp.where(usable, scores, -1e+30)
    highest = jnp.maximum(lax.optimization_barrier(jnp.max(masked, axis=-1)), scores_new)
    exp_terms = jnp.exp(masked - highest[..., None])
    exp_new = jnp.exp(scores_new - highest)
    totals = lax.optimization_barrier(jnp.sum(exp_terms, axis=-1)) + exp_new
    weights = (exp_terms / totals[..., None]).astype(jnp.bfloat16)
    weight_new = (exp_new / totals).astype(jnp.bfloat16)
    blended = jnp.einsum('bhgt,bthd->bhgd', weights.astype(jnp.float32), value_rows.astype(jnp.float32))
    blended = blended + weight_new.astype(jnp.float32)[..., None] * value_new.astype(jnp.float32)[:, :, None, :]
    return blended.astype(jnp.bfloat16).reshape(row_count, kv_heads * group_size * head_dim)

def expert_halves(rows_in, gate_w, up_w, down_w):
    half_width = gate_w.shape[1] // 2
    pieces = []
    for half_index in range(2):
        low_edge = half_index * half_width
        gate_part = jnp.dot(rows_in, gate_w[:, low_edge:low_edge + half_width], preferred_element_type=jnp.float32)
        up_part = jnp.dot(rows_in, up_w[:, low_edge:low_edge + half_width], preferred_element_type=jnp.float32)
        active = (jax.nn.silu(gate_part) * up_part).astype(jnp.bfloat16)
        partial_value = jnp.dot(active, down_w[low_edge:low_edge + half_width], preferred_element_type=jnp.float32).astype(jnp.bfloat16)
        pieces.append(lax.optimization_barrier(partial_value).astype(jnp.float32))
    return (pieces[0] + pieces[1]).astype(jnp.bfloat16)

def reference(hidden, queries, cache_keys, cache_values, new_keys, new_values, lengths, out_proj, norm_gain, expert_gate, expert_up, expert_down, expert_ids, gate_levels):
    blocks = ROWS // R_DEV
    packed = (queries.reshape(blocks, R_DEV, QH, HD), cache_keys.reshape(blocks, R_DEV, CACHE, KVH, HD), cache_values.reshape(blocks, R_DEV, CACHE, KVH, HD), new_keys.reshape(blocks, R_DEV, KVH, HD), new_values.reshape(blocks, R_DEV, KVH, HD), lengths.reshape(blocks, R_DEV))
    attended = lax.map(lambda items: attend_block(*items), packed).reshape(ROWS, QH * HD)
    residual = hidden.astype(jnp.float32) + jnp.dot(attended, out_proj, preferred_element_type=jnp.float32)
    normed = (residual * lax.rsqrt(lax.optimization_barrier(jnp.mean(residual * residual, axis=-1, keepdims=True)) + 1e-06) * norm_gain).astype(jnp.bfloat16)
    flat_ids = expert_ids.reshape(-1).astype(jnp.int32)
    entries = flat_ids.shape[0]
    one_hot = (flat_ids[:, None] == jnp.arange(EXPERTS, dtype=jnp.int32)[None, :]).astype(jnp.int32)
    ranks = (lax.optimization_barrier(jnp.sum(jnp.cumsum(one_hot, axis=0) * one_hot, axis=1)) - 1).astype(jnp.int32)
    slot_total = 2 * EXPERTS * CAP
    source_row = (jnp.arange(entries, dtype=jnp.int32) // TOPK).astype(jnp.int32)
    levels = gate_levels.astype(jnp.float32)
    shares = (levels / lax.optimization_barrier(jnp.sum(levels, axis=1, keepdims=True))).reshape(-1)
    table = jnp.full((EXPERTS, slot_total), ROWS, jnp.int32).at[flat_ids, ranks].set(source_row)
    share_table = jnp.zeros((EXPERTS, slot_total), jnp.float32).at[flat_ids, ranks].set(shares)
    padded = jnp.concatenate([normed, jnp.zeros((1, D), jnp.bfloat16)], axis=0)

    def run_expert(carry, packed_expert):
        rows_index, share_row, gate_w, up_w, down_w = packed_expert
        produced = expert_halves(padded[rows_index], gate_w, up_w, down_w)
        carry = carry.at[rows_index].add(share_row[:, None] * produced.astype(jnp.float32))
        return (carry, None)
    start_sum = jnp.zeros((ROWS + 1, D), jnp.float32)
    mixture, _ = lax.scan(run_expert, start_sum, (table, share_table, expert_gate, expert_up, expert_down))
    return (residual + mixture[:ROWS]).astype(jnp.bfloat16)
```

```python
import functools
import math

import jax
import jax.numpy as jnp
from jax import lax
from jax.experimental import pallas as pl
from jax.experimental.pallas import tpu as pltpu
from jax.sharding import PartitionSpec as P

MESH = pl.DeviceIdType.MESH


def attend_block(query_rows, key_rows, value_rows, key_new, value_new, valid_len):
    row_count = query_rows.shape[0]
    kv_heads = key_rows.shape[2]
    group_size = query_rows.shape[1] // kv_heads
    head_dim = query_rows.shape[2]
    scaling = 1.0 / math.sqrt(head_dim)
    query_f = query_rows.astype(jnp.float32).reshape(row_count, kv_heads, group_size, head_dim)
    scores = jnp.einsum("bhgd,bthd->bhgt", query_f, key_rows.astype(jnp.float32)) * scaling
    scores_new = jnp.einsum("bhgd,bhd->bhg", query_f, key_new.astype(jnp.float32)) * scaling
    positions = jnp.arange(key_rows.shape[1], dtype=jnp.int32)
    usable = (positions[None, :] < valid_len[:, None])[:, None, None, :]
    masked = jnp.where(usable, scores, -1e30)
    highest = jnp.maximum(jnp.max(masked, axis=-1), scores_new)
    exp_terms = jnp.exp(masked - highest[..., None])
    exp_new = jnp.exp(scores_new - highest)
    totals = jnp.sum(exp_terms, axis=-1) + exp_new
    weights = (exp_terms / totals[..., None]).astype(jnp.bfloat16)
    weight_new = (exp_new / totals).astype(jnp.bfloat16)
    blended = jnp.einsum("bhgt,bthd->bhgd", weights, value_rows, preferred_element_type=jnp.float32)
    blended = (
        blended
        + weight_new.astype(jnp.float32)[..., None] * value_new.astype(jnp.float32)[:, :, None, :]
    )
    return blended.astype(jnp.bfloat16).reshape(row_count, kv_heads * group_size * head_dim)


def expert_rows(rows_in, gate_w, up_w, down_w):
    gate_part = jnp.dot(rows_in, gate_w, preferred_element_type=jnp.float32)
    up_part = jnp.dot(rows_in, up_w, preferred_element_type=jnp.float32)
    active = (jax.nn.silu(gate_part) * up_part).astype(jnp.bfloat16)
    return jnp.dot(active, down_w, preferred_element_type=jnp.float32)


def slot_ranks(flat_ids, experts):
    one_hot = (flat_ids[:, None] == jnp.arange(experts, dtype=jnp.int32)[None, :]).astype(jnp.int32)
    return jnp.sum(jnp.cumsum(one_hot, axis=0) * one_hot, axis=1) - 1


def place_of(role, first, second, depth):
    head = first * (1 - role) + second * role
    low = second * (1 - role) + first * role
    return (role, 2 * depth + low, head)


def partner_depths(depth):
    return (depth, depth + 1 - 2 * (depth % 2), depth + 2 - 4 * (depth // 2), 3 - depth)


def layer_kernel(
    pieces,
    att_ref,
    hidden_ref,
    gain_ref,
    ids_ref,
    levels_ref,
    proj_hbm,
    gate_hbm,
    up_hbm,
    down_hbm,
    out_ref,
    gathered,
    proj_ref,
    gate_ref,
    up_ref,
    down_ref,
    col_out,
    col_in,
    residual_ref,
    token_ref,
    low_ref,
    high_ref,
    part_ref,
    core_in,
    first_out,
    first_in,
    second_out,
    second_in,
    depth_out,
    depth_in,
    weight_sems,
    att_send,
    att_recv,
    col_send,
    col_recv,
    tok_send,
    tok_recv,
    sum_send,
    sum_recv,
):
    role, dev, head = lax.axis_index("role"), lax.axis_index("dev"), lax.axis_index("head")
    group_count = gathered.shape[0]
    width = residual_ref.shape[1]
    half = width // 2
    member = dev * 2 + head
    members = group_count * 2
    low, depth = dev % 2, dev // 2
    first = head * (1 - role) + low * role
    second = low * (1 - role) + head * role
    depths = partner_depths(depth)
    other_core = (1 - role, dev, head)

    loads = [
        pltpu.make_async_copy(source, target, weight_sems.at[number])
        for number, (source, target) in enumerate(
            ((proj_hbm, proj_ref), (gate_hbm, gate_ref), (up_hbm, up_ref), (down_hbm, down_ref))
        )
    ]
    for load in loads:
        load.start()

    barrier = pltpu.get_barrier_semaphore()

    def greet(step, carry):
        target = (member + step) % members
        pl.semaphore_signal(
            barrier, inc=1, device_id=(role, target // 2, target % 2), device_id_type=MESH
        )
        return carry

    lax.fori_loop(1, members, greet, 0)
    pl.semaphore_signal(barrier, inc=1, device_id=other_core, device_id_type=MESH)
    gathered[dev] = att_ref[...]
    pl.semaphore_wait(barrier, members)

    def att_copy(depth_from, target, number):
        block = gathered.at[2 * depth_from + low]
        return pltpu.make_async_remote_copy(
            src_ref=block,
            dst_ref=block,
            send_sem=att_send.at[number],
            recv_sem=att_recv.at[number],
            device_id=target,
            device_id_type=MESH,
        )

    beside = (role, 2 * depth + 1 - low, head)
    along = [att_copy(depth, (role, 2 * depths[k] + low, head), k - 1) for k in (1, 2, 3)]
    across = [att_copy(depths[k], beside, 3 + k) for k in range(4)]
    across[0].start()
    for copy in along:
        copy.start()
    for k in (1, 2, 3):
        along[k - 1].wait_recv()
        across[k].start()
    for copy in across:
        copy.wait_recv()

    loads[0].wait()
    rows = gathered[...].reshape(group_count * gathered.shape[1], gathered.shape[2])
    columns = jnp.dot(rows, proj_ref[...], preferred_element_type=jnp.float32)
    col_width = columns.shape[1]
    tokens = residual_ref.shape[0]
    columns = columns.reshape(members, tokens, col_width)
    col_out[...] = jnp.concatenate(
        [columns[:, :, : col_width // 2], columns[:, :, col_width // 2 :]], axis=1
    ).astype(jnp.bfloat16)

    def col_copy(step):
        target = (member + step) % members
        return pltpu.make_async_remote_copy(
            src_ref=col_out.at[target],
            dst_ref=col_in.at[member],
            send_sem=col_send.at[step - 1],
            recv_sem=col_recv.at[step - 1],
            device_id=(role, target // 2, target % 2),
            device_id_type=MESH,
        )

    def col_start(step, carry):
        col_copy(step).start()
        return carry

    def col_arrive(step, carry):
        col_copy(step).wait_recv()
        return carry

    lax.fori_loop(1, members, col_start, 0)
    col_in[member] = col_out[member]
    lax.fori_loop(1, members, col_arrive, 0)

    for block in range(group_count):
        both = col_in[2 * block].astype(jnp.float32) + col_in[2 * block + 1].astype(jnp.float32)
        for side in range(2):
            edge = block * col_width + side * (col_width // 2)
            span = slice(edge, edge + col_width // 2)
            residual_ref[:, span] = (
                hidden_ref[:, span].astype(jnp.float32) + both[side * tokens : (side + 1) * tokens]
            )
    residual = residual_ref[...]
    square = jnp.sum(residual * residual, axis=-1, keepdims=True) / width
    normed = residual * lax.rsqrt(square + 1e-06) * gain_ref[...]
    lanes = lax.broadcasted_iota(jnp.int32, (tokens, 128), 1)
    named = jnp.zeros((tokens, 128), jnp.float32)
    for k in range(ids_ref.shape[1]):
        level = levels_ref[:, k : k + 1].astype(jnp.float32)
        named = named + jnp.where(lanes == ids_ref[:, k : k + 1], level, 0.0)
    slot = role * 16 + first * 8 + second * 4 + depth
    token_ref[slot, :, :half] = jnp.concatenate(
        [normed[:, :half], normed[:, half:]], axis=0
    ).astype(jnp.bfloat16)
    token_ref[slot, :, half:] = jnp.concatenate(
        [named, jnp.zeros((tokens, 128), jnp.float32)], axis=0
    ).astype(jnp.bfloat16)

    def token_copy(start, count, target, number):
        block = token_ref.at[pl.ds(start, count)]
        return pltpu.make_async_remote_copy(
            src_ref=block,
            dst_ref=block,
            send_sem=tok_send.at[number],
            recv_sem=tok_recv.at[number],
            device_id=target,
            device_id_type=MESH,
        )

    def slot_of(first_at, second_at, depth_at):
        return role * 16 + first_at * 8 + second_at * 4 + depth_at

    second_side = place_of(role, first, 1 - second, depth)
    first_side = place_of(role, 1 - first, second, depth)
    own = [slot_of(first, second, depths[k]) for k in range(4)]
    near = [slot_of(first, 1 - second, depths[k]) for k in range(4)]
    to_depth = [
        token_copy(own[0], 1, place_of(role, first, second, depths[k]), k - 1) for k in (1, 2, 3)
    ]
    to_second = [token_copy(own[k], 1, second_side, 3 + k) for k in range(4)]
    to_first = [token_copy(own[k], 1, first_side, 7 + k) for k in range(4)]
    to_first = to_first + [token_copy(near[k], 1, first_side, 11 + k) for k in range(4)]
    to_core = [
        token_copy(slot_of(*corner, 0), 4, other_core, 15 + number)
        for number, corner in enumerate(
            ((first, second), (first, 1 - second), (1 - first, second), (1 - first, 1 - second))
        )
    ]
    to_second[0].start()
    to_first[0].start()
    for copy in to_depth:
        copy.start()
    for k in (1, 2, 3):
        to_depth[k - 1].wait_recv()
        to_second[k].start()
        to_first[k].start()
    to_core[0].start()
    for k in range(4):
        to_second[k].wait_recv()
        to_first[4 + k].start()
    to_core[1].start()
    for k in range(4):
        to_first[k].wait_recv()
    to_core[2].start()
    for k in range(4, 8):
        to_first[k].wait_recv()
    to_core[3].start()
    for copy in to_core:
        copy.wait_recv()

    def unfold(pair, carry):
        one = token_ref[2 * pair, :, :half].astype(jnp.float32)
        two = token_ref[2 * pair + 1, :, :half].astype(jnp.float32)
        low_ref[pair] = jnp.concatenate([one[:tokens], two[:tokens]], axis=0).astype(jnp.bfloat16)
        high_ref[pair] = jnp.concatenate([one[tokens:], two[tokens:]], axis=0).astype(jnp.bfloat16)
        return carry

    pairs = low_ref.shape[0]
    lax.fori_loop(0, pairs, unfold, 0)
    total_rows = pairs * 2 * tokens
    table = token_ref[:, :, half:].astype(jnp.float32)[:, :tokens].reshape(total_rows, 128)
    mine = lax.broadcasted_iota(jnp.int32, (total_rows, 128), 1) == role * group_count + dev
    share = jnp.sum(jnp.where(mine, table, 0.0), axis=1, keepdims=True) / jnp.sum(
        table, axis=1, keepdims=True
    )
    left = low_ref[...].reshape(total_rows, half)
    right = high_ref[...].reshape(total_rows, half)

    def through(weight_ref):
        return jnp.dot(left, weight_ref[:half], preferred_element_type=jnp.float32) + jnp.dot(
            right, weight_ref[half:], preferred_element_type=jnp.float32
        )

    loads[1].wait()
    gate_part = through(gate_ref)
    loads[2].wait()
    up_part = through(up_ref)
    active = (gate_part / (1.0 + jnp.exp(-gate_part)) * up_part).astype(jnp.bfloat16)
    loads[3].wait()

    span_width = half // pieces

    def sum_copy(source, target, device, number):
        return pltpu.make_async_remote_copy(
            src_ref=source,
            dst_ref=target,
            send_sem=sum_send.at[number],
            recv_sem=sum_recv.at[number],
            device_id=device,
            device_id_type=MESH,
        )

    core_sums = [
        sum_copy(part_ref.at[p, pl.ds((1 - role) * 16, 16)], core_in.at[p], other_core, 6 * p)
        for p in range(pieces)
    ]
    first_sums = [
        sum_copy(first_out.at[p], first_in.at[p], first_side, 6 * p + 1) for p in range(pieces)
    ]
    second_sums = [
        sum_copy(second_out.at[p], second_in.at[p], second_side, 6 * p + 2) for p in range(pieces)
    ]
    depth_sums = [
        [
            sum_copy(
                depth_out.at[p, k - 1],
                depth_in.at[p, k - 1],
                place_of(role, first, second, depths[k]),
                6 * p + 2 + k,
            )
            for k in (1, 2, 3)
        ]
        for p in range(pieces)
    ]

    def produce(p):
        sides = []
        for side in range(2):
            edge = side * half + p * span_width
            product = jnp.dot(
                active, down_ref[:, edge : edge + span_width], preferred_element_type=jnp.float32
            )
            sides.append((product * share).reshape(2 * pairs, tokens, span_width))
        part_ref[p] = jnp.concatenate(sides, axis=1).astype(jnp.bfloat16)
        core_sums[p].start()

    def core_total(p, start, count):
        return part_ref[p, pl.ds(role * 16 + start, count)].astype(jnp.float32) + core_in[
            p, pl.ds(start, count)
        ].astype(jnp.float32)

    def pass_first(p):
        core_sums[p].wait_recv()
        first_out[p] = core_total(p, (1 - first) * 8, 8).astype(jnp.bfloat16)
        first_sums[p].start()

    def first_total(p, second_at, depth_at, count):
        start = second_at * 4 + depth_at
        return core_total(p, first * 8 + start, count) + first_in[p, pl.ds(start, count)].astype(
            jnp.float32
        )

    def pass_second(p):
        first_sums[p].wait_recv()
        second_out[p] = first_total(p, 1 - second, 0, 4).astype(jnp.bfloat16)
        second_sums[p].start()

    def second_total(p, depth_at):
        return first_total(p, second, depth_at, 1)[0] + second_in[p, depth_at].astype(jnp.float32)

    def pass_depth(p):
        second_sums[p].wait_recv()
        for k in (1, 2, 3):
            depth_out[p, k - 1] = second_total(p, depths[k]).astype(jnp.bfloat16)
            depth_sums[p][k - 1].start()

    def finish(p):
        total = second_total(p, depth)
        for k in range(3):
            depth_sums[p][k].wait_recv()
            total = total + depth_in[p, k].astype(jnp.float32)
        for side in range(2):
            edge = side * half + p * span_width
            span = slice(edge, edge + span_width)
            out_ref[:, span] = (
                residual_ref[:, span] + total[side * tokens : (side + 1) * tokens]
            ).astype(jnp.bfloat16)

    steps = (produce, pass_first, pass_second, pass_depth, finish)
    for turn in range(pieces + len(steps) - 1):
        for lag, step in enumerate(steps):
            if 0 <= turn - lag < pieces:
                step(turn - lag)

    def col_sent(step, carry):
        col_copy(step).wait_send()
        return carry

    lax.fori_loop(1, members, col_sent, 0)
    sent = along + across + to_depth + to_second + to_first + to_core
    sent = sent + core_sums + first_sums + second_sums
    for group in depth_sums:
        sent = sent + group
    for copy in sent:
        copy.wait_send()


def fused_layer(
    attended, hidden, norm_gain, expert_ids, gate_levels, out_proj, gate_w, up_w, down_w
):
    pieces = 4
    tokens, width = hidden.shape
    half = width // 2
    rows, inner = attended.shape
    col_width = out_proj.shape[1]
    dev_count = lax.axis_size("dev")
    hidden_units = gate_w.shape[1]
    span = half // pieces
    bf16 = jnp.bfloat16
    vmem = pl.BlockSpec(memory_space=pltpu.VMEM)
    anywhere = pl.BlockSpec(memory_space=pl.ANY)
    sems = pltpu.SemaphoreType.DMA
    return pl.pallas_call(
        functools.partial(layer_kernel, pieces),
        out_shape=jax.ShapeDtypeStruct((tokens, width), bf16),
        in_specs=[vmem] * 5 + [anywhere] * 4,
        out_specs=vmem,
        scratch_shapes=[
            pltpu.VMEM((dev_count, rows, inner), bf16),
            pltpu.VMEM(out_proj.shape, bf16),
            pltpu.VMEM((width, hidden_units), bf16),
            pltpu.VMEM((width, hidden_units), bf16),
            pltpu.VMEM((hidden_units, width), bf16),
            pltpu.VMEM((2 * dev_count, 2 * tokens, col_width // 2), bf16),
            pltpu.VMEM((2 * dev_count, 2 * tokens, col_width // 2), bf16),
            pltpu.VMEM((tokens, width), jnp.float32),
            pltpu.VMEM((4 * dev_count, 2 * tokens, half + 128), bf16),
            pltpu.VMEM((2 * dev_count, 2 * tokens, half), bf16),
            pltpu.VMEM((2 * dev_count, 2 * tokens, half), bf16),
            pltpu.VMEM((pieces, 32, 2 * tokens, span), bf16),
            pltpu.VMEM((pieces, 16, 2 * tokens, span), bf16),
            pltpu.VMEM((pieces, 8, 2 * tokens, span), bf16),
            pltpu.VMEM((pieces, 8, 2 * tokens, span), bf16),
            pltpu.VMEM((pieces, 4, 2 * tokens, span), bf16),
            pltpu.VMEM((pieces, 4, 2 * tokens, span), bf16),
            pltpu.VMEM((pieces, 3, 2 * tokens, span), bf16),
            pltpu.VMEM((pieces, 3, 2 * tokens, span), bf16),
            sems((4,)),
            sems((7,)),
            sems((7,)),
            sems((2 * dev_count - 1,)),
            sems((2 * dev_count - 1,)),
            sems((19,)),
            sems((19,)),
            sems((6 * pieces,)),
            sems((6 * pieces,)),
        ],
        compiler_params=pltpu.CompilerParams(
            collective_id=0, has_side_effects=True, vmem_limit_bytes=56 * 1024 * 1024
        ),
        cost_estimate=pl.CostEstimate(
            flops=3 * 2 * 256 * width * hidden_units, bytes_accessed=16 << 20, transcendentals=0
        ),
    )(
        attended,
        hidden,
        norm_gain.reshape(1, width),
        expert_ids,
        gate_levels,
        out_proj,
        gate_w,
        up_w,
        down_w,
    )


def on_device(
    hidden,
    queries,
    cache_keys,
    cache_values,
    new_keys,
    new_values,
    lengths,
    out_proj,
    norm_gain,
    expert_gate,
    expert_up,
    expert_down,
    expert_ids,
    gate_levels,
):
    attended = attend_block(queries, cache_keys, cache_values, new_keys, new_values, lengths)
    sizes = tuple(lax.axis_size(name) for name in ("role", "dev", "head"))
    if sizes == (2, 8, 2) and hidden.shape[0] == 8 and queries.shape[0] == 16:
        return fused_layer(
            attended,
            hidden,
            norm_gain,
            expert_ids,
            gate_levels,
            out_proj,
            expert_gate[0],
            expert_up[0],
            expert_down[0],
        )
    columns = jnp.dot(
        lax.all_gather(attended, "dev", axis=0, tiled=True),
        out_proj,
        preferred_element_type=jnp.float32,
    )
    dev_count = lax.axis_size("dev")
    head_count = lax.axis_size("head")
    experts = lax.axis_size("role") * dev_count
    col_width = out_proj.shape[1]
    width = dev_count * col_width
    projected = lax.all_to_all(columns, ("dev", "head"), split_axis=0, concat_axis=1, tiled=True)
    tokens = projected.shape[0]
    summed = jnp.sum(projected.reshape(tokens, dev_count, head_count, col_width), axis=2).reshape(
        tokens, width
    )
    residual = hidden.astype(jnp.float32) + summed
    normed = (
        residual
        * lax.rsqrt(jnp.mean(residual * residual, axis=-1, keepdims=True) + 1e-06)
        * norm_gain
    ).astype(jnp.bfloat16)
    top_k = expert_ids.shape[1]
    capacity = max(2, 2 * tokens * top_k // experts)
    own_ids = expert_ids.reshape(-1)
    own_ranks = slot_ranks(own_ids, experts)
    pair_rows, pair_ids = (
        lax.all_gather(normed, "head", axis=0, tiled=True),
        lax.all_gather(expert_ids, "head", axis=0, tiled=True),
    )
    pair_flat = pair_ids.reshape(head_count, tokens * top_k)
    pair_ranks = jax.vmap(lambda id_row: slot_ranks(id_row, experts))(pair_flat)
    pair_ranks = pair_ranks + capacity * jnp.arange(head_count, dtype=jnp.int32)[:, None]
    rows_from = jnp.arange(head_count * tokens * top_k, dtype=jnp.int32) // top_k
    outgoing = (
        jnp.zeros((experts, head_count * capacity, width), jnp.bfloat16)
        .at[pair_flat.reshape(-1), pair_ranks.reshape(-1)]
        .set(pair_rows[rows_from])
    )
    incoming = lax.all_to_all(outgoing, ("role", "dev"), split_axis=0, concat_axis=0, tiled=True)
    sources = incoming.shape[0]
    slot_total = incoming.shape[1]
    partial_value = expert_rows(
        incoming.reshape(sources * slot_total, width), expert_gate[0], expert_up[0], expert_down[0]
    )
    partial_value = partial_value.reshape(sources, slot_total, width).astype(jnp.bfloat16)
    arrived = lax.all_to_all(
        partial_value, ("role", "dev"), split_axis=0, concat_axis=0, tiled=True
    )
    arrived = (
        lax.psum_scatter(arrived, "head", scatter_dimension=1, tiled=True)
        .astype(jnp.float32)
        .astype(jnp.bfloat16)
    )
    picked = arrived[own_ids, own_ranks].astype(jnp.float32).reshape(tokens, top_k, width)
    levels = gate_levels.astype(jnp.float32)
    shares = levels / jnp.sum(levels, axis=1, keepdims=True)
    return (residual + jnp.sum(shares[..., None] * picked, axis=1)).astype(jnp.bfloat16)


def solution(mesh):
    placed = (
        P(("role", "dev", "head"), None),
        P(("role", "dev"), "head", None),
        P(("role", "dev"), None, "head", None),
        P(("role", "dev"), None, "head", None),
        P(("role", "dev"), "head", None),
        P(("role", "dev"), "head", None),
        P(("role", "dev")),
        P("head", "dev"),
        P(),
        P(("role", "dev"), None, "head"),
        P(("role", "dev"), None, "head"),
        P(("role", "dev"), "head", None),
        P(("role", "dev", "head"), None),
        P(("role", "dev", "head"), None),
    )
    return jax.shard_map(
        on_device,
        mesh=mesh,
        in_specs=placed,
        out_specs=P(("role", "dev", "head"), None),
        check_vma=False,
    )
```

```python
import functools
import math

import jax
import jax.numpy as jnp
from jax import lax
from jax.experimental import pallas as pl
from jax.experimental.pallas import tpu as pltpu
from jax.sharding import PartitionSpec as P

MESH = pl.DeviceIdType.MESH


def attend_block(query_rows, key_rows, value_rows, key_new, value_new, valid_len):
    row_count = query_rows.shape[0]
    kv_heads = key_rows.shape[2]
    group_size = query_rows.shape[1] // kv_heads
    head_dim = query_rows.shape[2]
    scaling = 1.0 / math.sqrt(head_dim)
    query_f = query_rows.astype(jnp.float32).reshape(row_count, kv_heads, group_size, head_dim)
    scores = jnp.einsum("bhgd,bthd->bhgt", query_f, key_rows.astype(jnp.float32)) * scaling
    scores_new = jnp.einsum("bhgd,bhd->bhg", query_f, key_new.astype(jnp.float32)) * scaling
    positions = jnp.arange(key_rows.shape[1], dtype=jnp.int32)
    usable = (positions[None, :] < valid_len[:, None])[:, None, None, :]
    masked = jnp.where(usable, scores, -1e30)
    highest = jnp.maximum(jnp.max(masked, axis=-1), scores_new)
    exp_terms = jnp.exp(masked - highest[..., None])
    exp_new = jnp.exp(scores_new - highest)
    totals = jnp.sum(exp_terms, axis=-1) + exp_new
    weights = (exp_terms / totals[..., None]).astype(jnp.bfloat16)
    weight_new = (exp_new / totals).astype(jnp.bfloat16)
    blended = jnp.einsum("bhgt,bthd->bhgd", weights, value_rows, preferred_element_type=jnp.float32)
    blended = (
        blended
        + weight_new.astype(jnp.float32)[..., None] * value_new.astype(jnp.float32)[:, :, None, :]
    )
    return blended.astype(jnp.bfloat16).reshape(row_count, kv_heads * group_size * head_dim)


def expert_rows(rows_in, gate_w, up_w, down_w):
    gate_part = jnp.dot(rows_in, gate_w, preferred_element_type=jnp.float32)
    up_part = jnp.dot(rows_in, up_w, preferred_element_type=jnp.float32)
    active = (jax.nn.silu(gate_part) * up_part).astype(jnp.bfloat16)
    return jnp.dot(active, down_w, preferred_element_type=jnp.float32)


def slot_ranks(flat_ids, experts):
    one_hot = (flat_ids[:, None] == jnp.arange(experts, dtype=jnp.int32)[None, :]).astype(jnp.int32)
    return jnp.sum(jnp.cumsum(one_hot, axis=0) * one_hot, axis=1) - 1


def place_of(role, first, second, depth):
    head = first * (1 - role) + second * role
    low = second * (1 - role) + first * role
    return (role, 2 * depth + low, head)


def partner_depths(depth):
    return (depth, depth + 1 - 2 * (depth % 2), depth + 2 - 4 * (depth // 2), 3 - depth)


def layer_kernel(
    pieces,
    query_ref,
    new_key_ref,
    new_value_ref,
    length_ref,
    keys_hbm,
    values_hbm,
    hidden_ref,
    gain_ref,
    ids_ref,
    levels_ref,
    proj_hbm,
    gate_hbm,
    up_hbm,
    down_hbm,
    out_ref,
    keys_ref,
    values_ref,
    att_ref,
    gathered,
    att_low,
    att_high,
    proj_ref,
    gate_ref,
    up_ref,
    down_ref,
    col_out,
    col_in,
    residual_ref,
    token_ref,
    low_ref,
    high_ref,
    active_ref,
    part_ref,
    core_in,
    first_out,
    first_in,
    second_out,
    second_in,
    depth_out,
    depth_in,
    weight_sems,
    att_send,
    att_recv,
    col_send,
    col_recv,
    tok_send,
    tok_recv,
    sum_send,
    sum_recv,
):
    role, dev, head = lax.axis_index("role"), lax.axis_index("dev"), lax.axis_index("head")
    group_count = gathered.shape[1]
    tokens = residual_ref.shape[0]
    width = residual_ref.shape[1]
    half = width // 2
    member = dev * 2 + head
    members = group_count * 2
    low, depth = dev % 2, dev // 2
    first = head * (1 - role) + low * role
    second = low * (1 - role) + head * role
    depths = partner_depths(depth)
    other_core = (1 - role, dev, head)

    loads = [
        pltpu.make_async_copy(source, target, weight_sems.at[number])
        for number, (source, target) in enumerate(
            (
                (proj_hbm, proj_ref),
                (gate_hbm, gate_ref),
                (up_hbm, up_ref),
                (down_hbm, down_ref),
                (keys_hbm, keys_ref),
                (values_hbm, values_ref),
            )
        )
    ]
    for load in loads[4:] + loads[:4]:
        load.start()

    barrier = pltpu.get_barrier_semaphore()

    def greet(step, carry):
        target = (member + step) % members
        pl.semaphore_signal(
            barrier, inc=1, device_id=(role, target // 2, target % 2), device_id_type=MESH
        )
        return carry

    lax.fori_loop(1, members, greet, 0)
    pl.semaphore_signal(barrier, inc=1, device_id=other_core, device_id_type=MESH)

    heads, head_dim = query_ref.shape[1:]
    slots = keys_ref.shape[1]
    shared = heads // 2
    scaling = 1.0 / math.sqrt(head_dim)
    column = lax.broadcasted_iota(jnp.int32, (heads, slots), 1)
    same_head = column % 2 == lax.broadcasted_iota(jnp.int32, (heads, slots), 0) // shared
    new_keys = new_key_ref[...].astype(jnp.float32)
    new_values = new_value_ref[...].astype(jnp.float32)

    def both_heads(rows, request):
        return jnp.concatenate(
            [
                jnp.broadcast_to(rows[2 * request + kv : 2 * request + kv + 1], (shared, head_dim))
                for kv in range(2)
            ],
            axis=0,
        )

    def attend(request):
        query = query_ref[request]
        scores = lax.dot_general(
            query,
            keys_ref[request],
            (((1,), (1,)), ((), ())),
            preferred_element_type=jnp.float32,
        )
        score_new = scaling * jnp.sum(
            query.astype(jnp.float32) * both_heads(new_keys, request), axis=1, keepdims=True
        )
        valid = same_head & (column < 2 * length_ref[request : request + 1, :])
        masked = jnp.where(valid, scores * scaling, -1e30)
        highest = jnp.maximum(jnp.max(masked, axis=1, keepdims=True), score_new)
        terms = jnp.exp(masked - highest)
        term_new = jnp.exp(score_new - highest)
        totals = jnp.sum(terms, axis=1, keepdims=True) + term_new
        weights = (terms / totals).astype(jnp.bfloat16)
        weight_new = (term_new / totals).astype(jnp.bfloat16).astype(jnp.float32)
        blended = jnp.dot(weights, values_ref[request], preferred_element_type=jnp.float32)
        att_ref[request * heads : (request + 1) * heads] = blended + weight_new * both_heads(
            new_values, request
        )

    def attend_half(part):
        for request in range(part * tokens, (part + 1) * tokens):
            attend(request)
        for j in range(shared):
            pair = [
                att_ref[pl.ds(part * tokens * heads + kv * shared + j, tokens, stride=heads), :]
                for kv in range(2)
            ]
            gathered[part, dev, :, j * head_dim : (j + 1) * head_dim] = jnp.concatenate(
                pair, axis=0
            ).astype(jnp.bfloat16)

    def att_copy(part, depth_from, target, number):
        block = gathered.at[part, 2 * depth_from + low]
        return pltpu.make_async_remote_copy(
            src_ref=block,
            dst_ref=block,
            send_sem=att_send.at[7 * part + number],
            recv_sem=att_recv.at[7 * part + number],
            device_id=target,
            device_id_type=MESH,
        )

    beside = (role, 2 * depth + 1 - low, head)
    along = [
        [att_copy(part, depth, (role, 2 * depths[k] + low, head), k - 1) for k in (1, 2, 3)]
        for part in range(2)
    ]
    across = [
        [att_copy(part, depths[k], beside, 3 + k) for k in range(4)] for part in range(2)
    ]
    loads[4].wait()
    loads[5].wait()
    for part in range(2):
        attend_half(part)
        if part == 0:
            pl.semaphore_wait(barrier, members)
        across[part][0].start()
        for copy in along[part]:
            copy.start()

    def unfold_att(block):
        one = gathered[0, block].astype(jnp.float32)
        two = gathered[1, block].astype(jnp.float32)
        att_low[block] = jnp.concatenate([one[:tokens], two[:tokens]], axis=0).astype(jnp.bfloat16)
        att_high[block] = jnp.concatenate([one[tokens:], two[tokens:]], axis=0).astype(
            jnp.bfloat16
        )

    for part in range(2):
        for k in (1, 2, 3):
            along[part][k - 1].wait_recv()
            across[part][k].start()
    for k in range(4):
        unfold_att(2 * depths[k] + low)
    for k in range(4):
        across[0][k].wait_recv()
    for k in range(4):
        across[1][k].wait_recv()
        unfold_att(2 * depths[k] + 1 - low)

    loads[0].wait()
    fold = att_low.shape[2]
    rows = group_count * 2 * tokens
    columns = jnp.dot(
        att_low[...].reshape(rows, fold), proj_ref[:fold], preferred_element_type=jnp.float32
    ) + jnp.dot(
        att_high[...].reshape(rows, fold), proj_ref[fold:], preferred_element_type=jnp.float32
    )
    col_width = columns.shape[1]
    columns = columns.reshape(members, tokens, col_width)
    col_out[...] = jnp.concatenate(
        [columns[:, :, : col_width // 2], columns[:, :, col_width // 2 :]], axis=1
    ).astype(jnp.bfloat16)

    def col_copy(step):
        target = (member + step) % members
        return pltpu.make_async_remote_copy(
            src_ref=col_out.at[target],
            dst_ref=col_in.at[member],
            send_sem=col_send.at[step - 1],
            recv_sem=col_recv.at[step - 1],
            device_id=(role, target // 2, target % 2),
            device_id_type=MESH,
        )

    def col_start(step, carry):
        col_copy(step).start()
        return carry

    def col_sent(step, carry):
        col_copy(step).wait_send()
        return carry

    def col_arrive(step, carry):
        col_copy(step).wait_recv()
        return carry

    lax.fori_loop(1, members, col_start, 0)
    col_in[member] = col_out[member]
    lax.fori_loop(1, members, col_arrive, 0)

    for block in range(group_count):
        both = col_in[2 * block].astype(jnp.float32) + col_in[2 * block + 1].astype(jnp.float32)
        for side in range(2):
            edge = block * col_width + side * (col_width // 2)
            span = slice(edge, edge + col_width // 2)
            residual_ref[:, span] = (
                hidden_ref[:, span].astype(jnp.float32) + both[side * tokens : (side + 1) * tokens]
            )
    residual = residual_ref[...]
    square = jnp.sum(residual * residual, axis=-1, keepdims=True) / width
    normed = residual * lax.rsqrt(square + 1e-06) * gain_ref[...]
    lanes = lax.broadcasted_iota(jnp.int32, (tokens, 128), 1)
    named = jnp.zeros((tokens, 128), jnp.float32)
    for k in range(ids_ref.shape[1]):
        level = levels_ref[:, k : k + 1].astype(jnp.float32)
        named = named + jnp.where(lanes == ids_ref[:, k : k + 1], level, 0.0)
    slot = role * 16 + first * 8 + second * 4 + depth
    token_ref[slot, :, :half] = jnp.concatenate(
        [normed[:, :half], normed[:, half:]], axis=0
    ).astype(jnp.bfloat16)
    token_ref[slot, :, half:] = jnp.concatenate(
        [named, jnp.zeros((tokens, 128), jnp.float32)], axis=0
    ).astype(jnp.bfloat16)

    def token_copy(start, count, target, number):
        block = token_ref.at[pl.ds(start, count)]
        return pltpu.make_async_remote_copy(
            src_ref=block,
            dst_ref=block,
            send_sem=tok_send.at[number],
            recv_sem=tok_recv.at[number],
            device_id=target,
            device_id_type=MESH,
        )

    def slot_of(first_at, second_at, depth_at):
        return role * 16 + first_at * 8 + second_at * 4 + depth_at

    second_side = place_of(role, first, 1 - second, depth)
    first_side = place_of(role, 1 - first, second, depth)
    own = [slot_of(first, second, depths[k]) for k in range(4)]
    near = [slot_of(first, 1 - second, depths[k]) for k in range(4)]
    to_depth = [
        token_copy(own[0], 1, place_of(role, first, second, depths[k]), k - 1) for k in (1, 2, 3)
    ]
    to_second = [token_copy(own[k], 1, second_side, 3 + k) for k in range(4)]
    to_first = [token_copy(own[k], 1, first_side, 7 + k) for k in range(4)]
    to_first = to_first + [token_copy(near[k], 1, first_side, 11 + k) for k in range(4)]
    to_core = [
        token_copy(slot_of(*corner, 0), 4, other_core, 15 + number)
        for number, corner in enumerate(
            ((first, second), (first, 1 - second), (1 - first, second), (1 - first, 1 - second))
        )
    ]
    to_second[0].start()
    to_first[0].start()
    for copy in to_depth:
        copy.start()
    for k in (1, 2, 3):
        to_depth[k - 1].wait_recv()
        to_second[k].start()
        to_first[k].start()
    to_core[0].start()

    def unfold(pair, carry):
        one = token_ref[2 * pair, :, :half].astype(jnp.float32)
        two = token_ref[2 * pair + 1, :, :half].astype(jnp.float32)
        low_ref[pair] = jnp.concatenate([one[:tokens], two[:tokens]], axis=0).astype(jnp.bfloat16)
        high_ref[pair] = jnp.concatenate([one[tokens:], two[tokens:]], axis=0).astype(jnp.bfloat16)
        return carry

    def unfold_from(role_at, first_at, second_at):
        start = role_at * 8 + first_at * 4 + second_at * 2
        lax.fori_loop(start, start + 2, unfold, 0)

    pairs = low_ref.shape[0]
    total_rows = pairs * 2 * tokens
    set_rows = total_rows // 4
    set_pairs = pairs // 4

    def expert_set(first_own, first_other):
        sides = []
        for ref in (low_ref, high_ref):
            both = [
                ref[pl.ds(role * 8 + first_own * 4, set_pairs)],
                ref[pl.ds((1 - role) * 8 + first_other * 4, set_pairs)],
            ]
            sides.append(jnp.concatenate(both, axis=0).reshape(2 * set_rows, half))

        def through(weight_ref):
            return jnp.dot(
                sides[0], weight_ref[:half], preferred_element_type=jnp.float32
            ) + jnp.dot(sides[1], weight_ref[half:], preferred_element_type=jnp.float32)

        gate_part = through(gate_ref)
        up_part = through(up_ref)
        active = (gate_part / (1.0 + jnp.exp(-gate_part)) * up_part).astype(jnp.bfloat16)
        active_ref[role * 2 + first_own] = active[:set_rows]
        active_ref[(1 - role) * 2 + first_other] = active[set_rows:]

    unfold_from(role, first, second)
    for k in range(4):
        to_second[k].wait_recv()
        to_first[4 + k].start()
    to_core[1].start()
    unfold_from(role, first, 1 - second)
    lax.fori_loop(1, members, col_sent, 0)
    for part in range(2):
        for copy in along[part] + across[part]:
            copy.wait_send()
    for load in loads[1:4]:
        load.wait()
    for k in range(4):
        to_first[k].wait_recv()
    to_core[2].start()
    unfold_from(role, 1 - first, second)
    to_core[0].wait_recv()
    unfold_from(1 - role, second, first)
    to_core[1].wait_recv()
    unfold_from(1 - role, second, 1 - first)
    expert_set(first, second)
    for k in range(4, 8):
        to_first[k].wait_recv()
    to_core[3].start()
    unfold_from(role, 1 - first, 1 - second)
    to_core[2].wait_recv()
    unfold_from(1 - role, 1 - second, first)
    to_core[3].wait_recv()
    unfold_from(1 - role, 1 - second, 1 - first)
    expert_set(1 - first, 1 - second)
    table = token_ref[:, :, half:].astype(jnp.float32)[:, :tokens].reshape(total_rows, 128)
    mine = lax.broadcasted_iota(jnp.int32, (total_rows, 128), 1) == role * group_count + dev
    share = jnp.sum(jnp.where(mine, table, 0.0), axis=1, keepdims=True) / jnp.sum(
        table, axis=1, keepdims=True
    )

    span_width = half // pieces

    def sum_copy(source, target, device, number):
        return pltpu.make_async_remote_copy(
            src_ref=source,
            dst_ref=target,
            send_sem=sum_send.at[number],
            recv_sem=sum_recv.at[number],
            device_id=device,
            device_id_type=MESH,
        )

    core_sums = [
        sum_copy(part_ref.at[p, pl.ds((1 - role) * 16, 16)], core_in.at[p], other_core, 6 * p)
        for p in range(pieces)
    ]
    first_sums = [
        sum_copy(first_out.at[p], first_in.at[p], first_side, 6 * p + 1) for p in range(pieces)
    ]
    second_sums = [
        sum_copy(second_out.at[p], second_in.at[p], second_side, 6 * p + 2) for p in range(pieces)
    ]
    depth_sums = [
        [
            sum_copy(
                depth_out.at[p, k - 1],
                depth_in.at[p, k - 1],
                place_of(role, first, second, depths[k]),
                6 * p + 2 + k,
            )
            for k in (1, 2, 3)
        ]
        for p in range(pieces)
    ]

    active_rows = active_ref[...].reshape(total_rows, active_ref.shape[2])

    def produce(p):
        sides = []
        for side in range(2):
            edge = side * half + p * span_width
            product = jnp.dot(
                active_rows, down_ref[:, edge : edge + span_width], preferred_element_type=jnp.float32
            )
            sides.append((product * share).reshape(2 * pairs, tokens, span_width))
        part_ref[p] = jnp.concatenate(sides, axis=1).astype(jnp.bfloat16)
        core_sums[p].start()

    def core_total(p, start, count):
        return part_ref[p, pl.ds(role * 16 + start, count)].astype(jnp.float32) + core_in[
            p, pl.ds(start, count)
        ].astype(jnp.float32)

    def pass_first(p):
        core_sums[p].wait_recv()
        first_out[p] = core_total(p, (1 - first) * 8, 8).astype(jnp.bfloat16)
        first_sums[p].start()

    def first_total(p, second_at, depth_at, count):
        start = second_at * 4 + depth_at
        return core_total(p, first * 8 + start, count) + first_in[p, pl.ds(start, count)].astype(
            jnp.float32
        )

    def pass_second(p):
        first_sums[p].wait_recv()
        second_out[p] = first_total(p, 1 - second, 0, 4).astype(jnp.bfloat16)
        second_sums[p].start()

    def second_total(p, depth_at):
        return first_total(p, second, depth_at, 1)[0] + second_in[p, depth_at].astype(jnp.float32)

    def pass_depth(p):
        second_sums[p].wait_recv()
        for k in (1, 2, 3):
            depth_out[p, k - 1] = second_total(p, depths[k]).astype(jnp.bfloat16)
            depth_sums[p][k - 1].start()

    def finish(p):
        total = second_total(p, depth)
        for k in range(3):
            depth_sums[p][k].wait_recv()
            total = total + depth_in[p, k].astype(jnp.float32)
        for side in range(2):
            edge = side * half + p * span_width
            span = slice(edge, edge + span_width)
            out_ref[:, span] = (
                residual_ref[:, span] + total[side * tokens : (side + 1) * tokens]
            )

    sent = to_depth + to_second + to_first + to_core

    def settle(p):
        share_of = -(-len(sent) // pieces)
        for copy in sent[p * share_of : (p + 1) * share_of]:
            copy.wait_send()
        for copy in (core_sums[p], first_sums[p], second_sums[p]):
            copy.wait_send()

    steps = (produce, pass_first, pass_second, pass_depth, finish)
    for turn in range(pieces + len(steps) - 1):
        for lag, step in enumerate(steps):
            if 0 <= turn - lag < pieces:
                step(turn - lag)
                if step is pass_depth:
                    settle(turn - lag)

    for group in depth_sums:
        for copy in group:
            copy.wait_send()


def fused_layer(
    queries,
    new_keys,
    new_values,
    lengths,
    cache_keys,
    cache_values,
    hidden,
    norm_gain,
    expert_ids,
    gate_levels,
    out_proj,
    gate_w,
    up_w,
    down_w,
):
    pieces = 4
    tokens, width = hidden.shape
    half = width // 2
    rows, heads, head_dim = queries.shape
    inner = heads * head_dim
    cached = cache_keys.shape[1] * cache_keys.shape[2]
    col_width = out_proj.shape[1]
    dev_count = lax.axis_size("dev")
    hidden_units = gate_w.shape[1]
    span = half // pieces
    bf16 = jnp.bfloat16
    vmem = pl.BlockSpec(memory_space=pltpu.VMEM)
    anywhere = pl.BlockSpec(memory_space=pl.ANY)
    sems = pltpu.SemaphoreType.DMA
    out = pl.pallas_call(
        functools.partial(layer_kernel, pieces),
        out_shape=jax.ShapeDtypeStruct((tokens, width), jnp.float32),
        in_specs=[vmem] * 4 + [anywhere] * 2 + [vmem] * 4 + [anywhere] * 4,
        out_specs=vmem,
        scratch_shapes=[
            pltpu.VMEM((rows, cached, head_dim), bf16),
            pltpu.VMEM((rows, cached, head_dim), bf16),
            pltpu.VMEM((rows * heads, head_dim), jnp.float32),
            pltpu.VMEM((2, dev_count, rows, inner // 2), bf16),
            pltpu.VMEM((dev_count, rows, inner // 2), bf16),
            pltpu.VMEM((dev_count, rows, inner // 2), bf16),
            pltpu.VMEM(out_proj.shape, bf16),
            pltpu.VMEM((width, hidden_units), bf16),
            pltpu.VMEM((width, hidden_units), bf16),
            pltpu.VMEM((hidden_units, width), bf16),
            pltpu.VMEM((2 * dev_count, 2 * tokens, col_width // 2), bf16),
            pltpu.VMEM((2 * dev_count, 2 * tokens, col_width // 2), bf16),
            pltpu.VMEM((tokens, width), jnp.float32),
            pltpu.VMEM((4 * dev_count, 2 * tokens, half + 128), bf16),
            pltpu.VMEM((2 * dev_count, 2 * tokens, half), bf16),
            pltpu.VMEM((2 * dev_count, 2 * tokens, half), bf16),
            pltpu.VMEM((4, 8 * tokens, hidden_units), bf16),
            pltpu.VMEM((pieces, 32, 2 * tokens, span), bf16),
            pltpu.VMEM((pieces, 16, 2 * tokens, span), bf16),
            pltpu.VMEM((pieces, 8, 2 * tokens, span), bf16),
            pltpu.VMEM((pieces, 8, 2 * tokens, span), bf16),
            pltpu.VMEM((pieces, 4, 2 * tokens, span), bf16),
            pltpu.VMEM((pieces, 4, 2 * tokens, span), bf16),
            pltpu.VMEM((pieces, 3, 2 * tokens, span), bf16),
            pltpu.VMEM((pieces, 3, 2 * tokens, span), bf16),
            sems((6,)),
            sems((14,)),
            sems((14,)),
            sems((2 * dev_count - 1,)),
            sems((2 * dev_count - 1,)),
            sems((19,)),
            sems((19,)),
            sems((6 * pieces,)),
            sems((6 * pieces,)),
        ],
        compiler_params=pltpu.CompilerParams(
            collective_id=0, has_side_effects=True, vmem_limit_bytes=56 * 1024 * 1024
        ),
        cost_estimate=pl.CostEstimate(
            flops=3 * 2 * 256 * width * hidden_units, bytes_accessed=16 << 20, transcendentals=0
        ),
    )(
        queries,
        new_keys.reshape(2 * rows, head_dim),
        new_values.reshape(2 * rows, head_dim),
        lengths.reshape(rows, 1),
        cache_keys.reshape(rows, cached, head_dim),
        cache_values.reshape(rows, cached, head_dim),
        hidden,
        norm_gain.reshape(1, width),
        expert_ids,
        gate_levels,
        out_proj,
        gate_w,
        up_w,
        down_w,
    )
    return out.astype(bf16)


def on_device(
    hidden,
    queries,
    cache_keys,
    cache_values,
    new_keys,
    new_values,
    lengths,
    out_proj,
    norm_gain,
    expert_gate,
    expert_up,
    expert_down,
    expert_ids,
    gate_levels,
):
    sizes = tuple(lax.axis_size(name) for name in ("role", "dev", "head"))
    if sizes == (2, 8, 2) and hidden.shape[0] == 8 and queries.shape[0] == 16:
        return fused_layer(
            queries,
            new_keys,
            new_values,
            lengths,
            cache_keys,
            cache_values,
            hidden,
            norm_gain,
            expert_ids,
            gate_levels,
            out_proj,
            expert_gate[0],
            expert_up[0],
            expert_down[0],
        )
    attended = attend_block(queries, cache_keys, cache_values, new_keys, new_values, lengths)
    columns = jnp.dot(
        lax.all_gather(attended, "dev", axis=0, tiled=True),
        out_proj,
        preferred_element_type=jnp.float32,
    )
    dev_count = lax.axis_size("dev")
    head_count = lax.axis_size("head")
    experts = lax.axis_size("role") * dev_count
    col_width = out_proj.shape[1]
    width = dev_count * col_width
    projected = lax.all_to_all(columns, ("dev", "head"), split_axis=0, concat_axis=1, tiled=True)
    tokens = projected.shape[0]
    summed = jnp.sum(projected.reshape(tokens, dev_count, head_count, col_width), axis=2).reshape(
        tokens, width
    )
    residual = hidden.astype(jnp.float32) + summed
    normed = (
        residual
        * lax.rsqrt(jnp.mean(residual * residual, axis=-1, keepdims=True) + 1e-06)
        * norm_gain
    ).astype(jnp.bfloat16)
    top_k = expert_ids.shape[1]
    capacity = max(2, 2 * tokens * top_k // experts)
    own_ids = expert_ids.reshape(-1)
    own_ranks = slot_ranks(own_ids, experts)
    pair_rows, pair_ids = (
        lax.all_gather(normed, "head", axis=0, tiled=True),
        lax.all_gather(expert_ids, "head", axis=0, tiled=True),
    )
    pair_flat = pair_ids.reshape(head_count, tokens * top_k)
    pair_ranks = jax.vmap(lambda id_row: slot_ranks(id_row, experts))(pair_flat)
    pair_ranks = pair_ranks + capacity * jnp.arange(head_count, dtype=jnp.int32)[:, None]
    rows_from = jnp.arange(head_count * tokens * top_k, dtype=jnp.int32) // top_k
    outgoing = (
        jnp.zeros((experts, head_count * capacity, width), jnp.bfloat16)
        .at[pair_flat.reshape(-1), pair_ranks.reshape(-1)]
        .set(pair_rows[rows_from])
    )
    incoming = lax.all_to_all(outgoing, ("role", "dev"), split_axis=0, concat_axis=0, tiled=True)
    sources = incoming.shape[0]
    slot_total = incoming.shape[1]
    partial_value = expert_rows(
        incoming.reshape(sources * slot_total, width), expert_gate[0], expert_up[0], expert_down[0]
    )
    partial_value = partial_value.reshape(sources, slot_total, width).astype(jnp.bfloat16)
    arrived = lax.all_to_all(
        partial_value, ("role", "dev"), split_axis=0, concat_axis=0, tiled=True
    )
    arrived = (
        lax.psum_scatter(arrived, "head", scatter_dimension=1, tiled=True)
        .astype(jnp.float32)
        .astype(jnp.bfloat16)
    )
    picked = arrived[own_ids, own_ranks].astype(jnp.float32).reshape(tokens, top_k, width)
    levels = gate_levels.astype(jnp.float32)
    shares = levels / jnp.sum(levels, axis=1, keepdims=True)
    return (residual + jnp.sum(shares[..., None] * picked, axis=1)).astype(jnp.bfloat16)


def solution(mesh):
    placed = (
        P(("role", "dev", "head"), None),
        P(("role", "dev"), "head", None),
        P(("role", "dev"), None, "head", None),
        P(("role", "dev"), None, "head", None),
        P(("role", "dev"), "head", None),
        P(("role", "dev"), "head", None),
        P(("role", "dev")),
        P("head", "dev"),
        P(),
        P(("role", "dev"), None, "head"),
        P(("role", "dev"), None, "head"),
        P(("role", "dev"), "head", None),
        P(("role", "dev", "head"), None),
        P(("role", "dev", "head"), None),
    )
    return jax.shard_map(
        on_device,
        mesh=mesh,
        in_specs=placed,
        out_specs=P(("role", "dev", "head"), None),
        check_vma=False,
    )
```

```python
import functools
import math

import jax
import jax.numpy as jnp
from jax import lax
from jax.experimental import pallas as pl
from jax.experimental.pallas import tpu as pltpu
from jax.sharding import PartitionSpec as P

MESH = pl.DeviceIdType.MESH


def attend_block(query_rows, key_rows, value_rows, key_new, value_new, valid_len):
    row_count = query_rows.shape[0]
    kv_heads = key_rows.shape[2]
    group_size = query_rows.shape[1] // kv_heads
    head_dim = query_rows.shape[2]
    scaling = 1.0 / math.sqrt(head_dim)
    query_f = query_rows.astype(jnp.float32).reshape(row_count, kv_heads, group_size, head_dim)
    scores = jnp.einsum("bhgd,bthd->bhgt", query_f, key_rows.astype(jnp.float32)) * scaling
    scores_new = jnp.einsum("bhgd,bhd->bhg", query_f, key_new.astype(jnp.float32)) * scaling
    positions = jnp.arange(key_rows.shape[1], dtype=jnp.int32)
    usable = (positions[None, :] < valid_len[:, None])[:, None, None, :]
    masked = jnp.where(usable, scores, -1e30)
    highest = jnp.maximum(jnp.max(masked, axis=-1), scores_new)
    exp_terms = jnp.exp(masked - highest[..., None])
    exp_new = jnp.exp(scores_new - highest)
    totals = jnp.sum(exp_terms, axis=-1) + exp_new
    weights = (exp_terms / totals[..., None]).astype(jnp.bfloat16)
    weight_new = (exp_new / totals).astype(jnp.bfloat16)
    blended = jnp.einsum("bhgt,bthd->bhgd", weights, value_rows, preferred_element_type=jnp.float32)
    blended = (
        blended
        + weight_new.astype(jnp.float32)[..., None] * value_new.astype(jnp.float32)[:, :, None, :]
    )
    return blended.astype(jnp.bfloat16).reshape(row_count, kv_heads * group_size * head_dim)


def expert_rows(rows_in, gate_w, up_w, down_w):
    gate_part = jnp.dot(rows_in, gate_w, preferred_element_type=jnp.float32)
    up_part = jnp.dot(rows_in, up_w, preferred_element_type=jnp.float32)
    active = (jax.nn.silu(gate_part) * up_part).astype(jnp.bfloat16)
    return jnp.dot(active, down_w, preferred_element_type=jnp.float32)


def slot_ranks(flat_ids, experts):
    one_hot = (flat_ids[:, None] == jnp.arange(experts, dtype=jnp.int32)[None, :]).astype(jnp.int32)
    return jnp.sum(jnp.cumsum(one_hot, axis=0) * one_hot, axis=1) - 1


def partner_depths(depth):
    return (depth, depth + 1 - 2 * (depth % 2), depth + 2 - 4 * (depth // 2), 3 - depth)


def layer_kernel(
    pieces,
    query_ref,
    new_key_ref,
    new_value_ref,
    length_ref,
    keys_hbm,
    values_hbm,
    hidden_ref,
    gain_ref,
    ids_ref,
    levels_ref,
    proj_hbm,
    gate_hbm,
    up_hbm,
    down_hbm,
    out_ref,
    keys_ref,
    values_ref,
    att_ref,
    gathered,
    att_low,
    att_high,
    proj_ref,
    gate_ref,
    up_ref,
    down_ref,
    col_out,
    col_in,
    residual_ref,
    token_ref,
    low_ref,
    high_ref,
    part_ref,
    core_in,
    near_out,
    near_in,
    head_out,
    head_in,
    depth_out,
    depth_in,
    weight_sems,
    att_send,
    att_recv,
    col_send,
    col_recv,
    tok_send,
    tok_recv,
    sum_send,
    sum_recv,
):
    role, dev, head = lax.axis_index("role"), lax.axis_index("dev"), lax.axis_index("head")
    group_count = gathered.shape[1]
    tokens = residual_ref.shape[0]
    width = residual_ref.shape[1]
    half = width // 2
    col_width = proj_ref.shape[1]
    member = dev * 2 + head
    members = group_count * 2
    low, depth = dev % 2, dev // 2
    depths = partner_depths(depth)
    other_core = (1 - role, dev, head)

    loads = [
        pltpu.make_async_copy(source, target, weight_sems.at[number])
        for number, (source, target) in enumerate(
            (
                (proj_hbm, proj_ref),
                (gate_hbm, gate_ref),
                (up_hbm, up_ref),
                (down_hbm, down_ref),
                (keys_hbm, keys_ref),
                (values_hbm, values_ref),
            )
        )
    ]
    for load in loads[4:] + loads[:4]:
        load.start()

    barrier = pltpu.get_barrier_semaphore()

    def greet(step, carry):
        target = (member + step) % members
        pl.semaphore_signal(
            barrier, inc=1, device_id=(role, target // 2, target % 2), device_id_type=MESH
        )
        return carry

    lax.fori_loop(1, members, greet, 0)
    pl.semaphore_signal(barrier, inc=1, device_id=other_core, device_id_type=MESH)

    heads, head_dim = query_ref.shape[1:]
    slots = keys_ref.shape[1]
    shared = heads // 2
    scaling = 1.0 / math.sqrt(head_dim)
    column = lax.broadcasted_iota(jnp.int32, (heads, slots), 1)
    same_head = column % 2 == lax.broadcasted_iota(jnp.int32, (heads, slots), 0) // shared
    new_keys = new_key_ref[...].astype(jnp.float32)
    new_values = new_value_ref[...].astype(jnp.float32)

    def both_heads(rows, request):
        return jnp.concatenate(
            [
                jnp.broadcast_to(rows[2 * request + kv : 2 * request + kv + 1], (shared, head_dim))
                for kv in range(2)
            ],
            axis=0,
        )

    def attend(request):
        query = query_ref[request]
        scores = lax.dot_general(
            query,
            keys_ref[request],
            (((1,), (1,)), ((), ())),
            preferred_element_type=jnp.float32,
        )
        score_new = scaling * jnp.sum(
            query.astype(jnp.float32) * both_heads(new_keys, request), axis=1, keepdims=True
        )
        valid = same_head & (column < 2 * length_ref[request])
        masked = jnp.where(valid, scores * scaling, -1e30)
        highest = jnp.maximum(jnp.max(masked, axis=1, keepdims=True), score_new)
        terms = jnp.exp(masked - highest)
        term_new = jnp.exp(score_new - highest)
        totals = jnp.sum(terms, axis=1, keepdims=True) + term_new
        weights = (terms / totals).astype(jnp.bfloat16)
        weight_new = (term_new / totals).astype(jnp.bfloat16).astype(jnp.float32)
        blended = jnp.dot(weights, values_ref[request], preferred_element_type=jnp.float32)
        att_ref[request * heads : (request + 1) * heads] = blended + weight_new * both_heads(
            new_values, request
        )

    def attend_half(part):
        for request in range(part * tokens, (part + 1) * tokens):
            attend(request)
        for j in range(shared):
            pair = [
                att_ref[pl.ds(part * tokens * heads + kv * shared + j, tokens, stride=heads), :]
                for kv in range(2)
            ]
            gathered[part, dev, :, j * head_dim : (j + 1) * head_dim] = jnp.concatenate(
                pair, axis=0
            ).astype(jnp.bfloat16)

    def att_copy(part, depth_from, target, number):
        block = gathered.at[part, 2 * depth_from + low]
        return pltpu.make_async_remote_copy(
            src_ref=block,
            dst_ref=block,
            send_sem=att_send.at[7 * part + number],
            recv_sem=att_recv.at[7 * part + number],
            device_id=target,
            device_id_type=MESH,
        )

    beside = (role, 2 * depth + 1 - low, head)
    along = [
        [att_copy(part, depth, (role, 2 * depths[k] + low, head), k - 1) for k in (1, 2, 3)]
        for part in range(2)
    ]
    across = [
        [att_copy(part, depths[k], beside, 3 + k) for k in range(4)] for part in range(2)
    ]
    loads[4].wait()
    loads[5].wait()
    for part in range(2):
        attend_half(part)
        if part == 0:
            pl.semaphore_wait(barrier, members)
        across[part][0].start()
        for copy in along[part]:
            copy.start()

    fold = att_low.shape[3]

    def project(part):
        for pair in range(group_count // 2):
            one = gathered[part, 2 * pair].astype(jnp.float32)
            two = gathered[part, 2 * pair + 1].astype(jnp.float32)
            att_low[part, pair] = jnp.concatenate([one[:tokens], two[:tokens]], axis=0).astype(
                jnp.bfloat16
            )
            att_high[part, pair] = jnp.concatenate([one[tokens:], two[tokens:]], axis=0).astype(
                jnp.bfloat16
            )
        rows = group_count * tokens
        columns = jnp.dot(
            att_low[part].reshape(rows, fold),
            proj_ref[:fold],
            preferred_element_type=jnp.float32,
        ) + jnp.dot(
            att_high[part].reshape(rows, fold),
            proj_ref[fold:],
            preferred_element_type=jnp.float32,
        )
        columns = columns.reshape(group_count, tokens, col_width)
        col_out[part] = jnp.concatenate(
            [columns[:, :, : col_width // 2], columns[:, :, col_width // 2 :]], axis=1
        ).astype(jnp.bfloat16)

    def col_copy(step, to_head, number):
        target = (dev + step) % group_count
        return pltpu.make_async_remote_copy(
            src_ref=col_out.at[to_head, target],
            dst_ref=col_in.at[member],
            send_sem=col_send.at[number],
            recv_sem=col_recv.at[number],
            device_id=(role, target, to_head),
            device_id_type=MESH,
        )

    def same_col(step):
        return col_copy(step, head, step - 1)

    def other_col(step):
        return col_copy(step, 1 - head, group_count - 1 + step)

    def over_cols(act):
        def same_step(step, carry):
            act(same_col(step))
            return carry

        def other_step(step, carry):
            act(other_col(step))
            return carry

        return (
            lambda: lax.fori_loop(1, group_count, same_step, 0),
            lambda: lax.fori_loop(0, group_count, other_step, 0),
        )

    start_same, start_other = over_cols(lambda copy: copy.start())
    arrive_same, arrive_other = over_cols(lambda copy: copy.wait_recv())
    sent_same, sent_other = over_cols(lambda copy: copy.wait_send())

    def send_columns(part):
        @pl.when(head == part)
        def _():
            start_same()
            col_in[member] = col_out[part, dev]

        @pl.when(head != part)
        def _():
            start_other()

    def token_copy(start, count, target, number):
        block = token_ref.at[pl.ds(start, count)]
        return pltpu.make_async_remote_copy(
            src_ref=block,
            dst_ref=block,
            send_sem=tok_send.at[number],
            recv_sem=tok_recv.at[number],
            device_id=target,
            device_id_type=MESH,
        )

    def slot_of(head_at, low_at, depth_at):
        return role * 16 + head_at * 8 + low_at * 4 + depth_at

    other_head = (role, dev, 1 - head)
    own_slot = slot_of(head, low, depth)
    to_depth = [
        token_copy(own_slot, 1, (role, 2 * depths[k] + low, head), k - 1) for k in (1, 2, 3)
    ]
    to_head = [token_copy(slot_of(head, low, depths[k]), 1, other_head, 3 + k) for k in range(4)]
    to_near = [
        [token_copy(slot_of(h, low, depths[k]), 1, beside, 7 + 4 * h + k) for k in range(4)]
        for h in range(2)
    ]
    to_core = [
        [token_copy(slot_of(h, low_at, 0), 4, other_core, 15 + 2 * h + g)
         for g, low_at in enumerate((low, 1 - low))]
        for h in range(2)
    ]

    def begin_tokens():
        arrive_same()
        arrive_other()
        for block in range(group_count):
            both = col_in[2 * block].astype(jnp.float32) + col_in[2 * block + 1].astype(
                jnp.float32
            )
            for side in range(2):
                edge = block * col_width + side * (col_width // 2)
                span = slice(edge, edge + col_width // 2)
                residual_ref[:, span] = (
                    hidden_ref[:, span].astype(jnp.float32)
                    + both[side * tokens : (side + 1) * tokens]
                )
        residual = residual_ref[...]
        square = jnp.sum(residual * residual, axis=-1, keepdims=True) / width
        normed = residual * lax.rsqrt(square + 1e-06) * gain_ref[...]
        lanes = lax.broadcasted_iota(jnp.int32, (tokens, 128), 1)
        named = jnp.zeros((tokens, 128), jnp.float32)
        for k in range(ids_ref.shape[1]):
            level = levels_ref[:, k : k + 1].astype(jnp.float32)
            named = named + jnp.where(lanes == ids_ref[:, k : k + 1], level, 0.0)
        token_ref[own_slot, :, :half] = jnp.concatenate(
            [normed[:, :half], normed[:, half:]], axis=0
        ).astype(jnp.bfloat16)
        token_ref[own_slot, :, half:] = jnp.concatenate(
            [named, jnp.zeros((tokens, 128), jnp.float32)], axis=0
        ).astype(jnp.bfloat16)
        for copy in to_depth:
            copy.start()
        to_head[0].start()

    def relay(h):
        @pl.when(head == h)
        def _():
            to_near[h][0].start()
            for k in (1, 2, 3):
                to_depth[k - 1].wait_recv()
                to_head[k].start()
                to_near[h][k].start()

        @pl.when(head != h)
        def _():
            for k in range(4):
                to_head[k].wait_recv()
                to_near[h][k].start()

        to_core[h][0].start()

    def unfold(pair, carry):
        one = token_ref[2 * pair, :, :half].astype(jnp.float32)
        two = token_ref[2 * pair + 1, :, :half].astype(jnp.float32)
        low_ref[pair] = jnp.concatenate([one[:tokens], two[:tokens]], axis=0).astype(jnp.bfloat16)
        high_ref[pair] = jnp.concatenate([one[tokens:], two[tokens:]], axis=0).astype(jnp.bfloat16)
        return carry

    def unfold_from(role_at, h, low_at):
        start = role_at * 8 + h * 4 + low_at * 2
        lax.fori_loop(start, start + 2, unfold, 0)

    def collect(h):
        unfold_from(role, h, low)
        for k in range(4):
            to_near[h][k].wait_recv()
        to_core[h][1].start()
        unfold_from(role, h, 1 - low)
        to_core[h][0].wait_recv()
        unfold_from(1 - role, h, low)
        to_core[h][1].wait_recv()
        unfold_from(1 - role, h, 1 - low)

    set_rows = 2 * group_count * tokens

    def expert_set(h):
        sides = [
            jnp.concatenate([ref[h * 4 : h * 4 + 4], ref[8 + h * 4 : 12 + h * 4]], axis=0).reshape(
                set_rows, half
            )
            for ref in (low_ref, high_ref)
        ]

        def through(weight_ref):
            return jnp.dot(
                sides[0], weight_ref[:half], preferred_element_type=jnp.float32
            ) + jnp.dot(sides[1], weight_ref[half:], preferred_element_type=jnp.float32)

        gate_part = through(gate_ref)
        up_part = through(up_ref)
        active = (gate_part / (1.0 + jnp.exp(-gate_part)) * up_part).astype(jnp.bfloat16)
        table = jnp.concatenate(
            [token_ref[h * 8 : h * 8 + 8, :, half:], token_ref[16 + h * 8 : 24 + h * 8, :, half:]],
            axis=0,
        )
        table = table.astype(jnp.float32)[:, :tokens].reshape(set_rows, 128)
        mine = lax.broadcasted_iota(jnp.int32, (set_rows, 128), 1) == role * group_count + dev
        share = jnp.sum(jnp.where(mine, table, 0.0), axis=1, keepdims=True) / jnp.sum(
            table, axis=1, keepdims=True
        )
        return active, share

    span_width = half // pieces

    def sum_copy(source, target, device, number):
        return pltpu.make_async_remote_copy(
            src_ref=source,
            dst_ref=target,
            send_sem=sum_send.at[number],
            recv_sem=sum_recv.at[number],
            device_id=device,
            device_id_type=MESH,
        )

    core_sums = [
        [
            sum_copy(part_ref.at[h, p, 1 - role], core_in.at[h, p], other_core, h * pieces + p)
            for p in range(pieces)
        ]
        for h in range(2)
    ]
    near_sums = [
        [
            sum_copy(near_out.at[h, p], near_in.at[h, p], beside, (2 + h) * pieces + p)
            for p in range(pieces)
        ]
        for h in range(2)
    ]
    head_sums = [
        sum_copy(head_out.at[p], head_in.at[p], other_head, 4 * pieces + p) for p in range(pieces)
    ]
    depth_sums = [
        [
            sum_copy(
                depth_out.at[p, k - 1],
                depth_in.at[p, k - 1],
                (role, 2 * depths[k] + low, head),
                (4 + k) * pieces + p,
            )
            for k in (1, 2, 3)
        ]
        for p in range(pieces)
    ]

    def produce(h, p, active, share):
        sides = []
        for side in range(2):
            edge = side * half + p * span_width
            product = jnp.dot(
                active, down_ref[:, edge : edge + span_width], preferred_element_type=jnp.float32
            )
            sides.append((product * share).reshape(2, group_count, tokens, span_width))
        part_ref[h, p] = jnp.concatenate(sides, axis=2).astype(jnp.bfloat16)
        core_sums[h][p].start()

    def core_total(h, p, start, count):
        return part_ref[h, p, role, pl.ds(start, count)].astype(jnp.float32) + core_in[
            h, p, pl.ds(start, count)
        ].astype(jnp.float32)

    def near_total(h, p, depth_at, count):
        return core_total(h, p, low * 4 + depth_at, count) + near_in[
            h, p, pl.ds(depth_at, count)
        ].astype(jnp.float32)

    def head_total(h, p, depth_at):
        return near_total(h, p, depth_at, 1)[0] + head_in[p, depth_at].astype(jnp.float32)

    def pass_near(h, p):
        core_sums[h][p].wait_recv()
        near_out[h, p] = core_total(h, p, (1 - low) * 4, 4).astype(jnp.bfloat16)
        near_sums[h][p].start()

    def pass_head(h, p):
        near_sums[h][p].wait_recv()

        @pl.when(head != h)
        def _():
            head_out[p] = near_total(h, p, 0, 4).astype(jnp.bfloat16)
            head_sums[p].start()

    def pass_depth(h, p):
        @pl.when(head == h)
        def _():
            head_sums[p].wait_recv()
            for k in (1, 2, 3):
                depth_out[p, k - 1] = head_total(h, p, depths[k]).astype(jnp.bfloat16)
                depth_sums[p][k - 1].start()

    def finish(h, p):
        @pl.when(head == h)
        def _():
            total = head_total(h, p, depth)
            for k in range(3):
                depth_sums[p][k].wait_recv()
                total = total + depth_in[p, k].astype(jnp.float32)
            for side in range(2):
                edge = side * half + p * span_width
                span = slice(edge, edge + span_width)
                out_ref[:, span] = (
                    residual_ref[:, span] + total[side * tokens : (side + 1) * tokens]
                )

    for k in (1, 2, 3):
        along[0][k - 1].wait_recv()
        across[0][k].start()
    loads[0].wait()
    for k in range(4):
        across[0][k].wait_recv()
    along[1][0].wait_recv()
    across[1][1].start()
    project(0)
    send_columns(0)
    for k in (2, 3):
        along[1][k - 1].wait_recv()
        across[1][k].start()

    @pl.when(head == 0)
    def _():
        begin_tokens()

    for k in range(4):
        across[1][k].wait_recv()
    project(1)
    send_columns(1)
    relay(0)

    @pl.when(head == 1)
    def _():
        begin_tokens()

    for load in loads[1:4]:
        load.wait()
    collect(0)
    active, share = expert_set(0)
    for p in range(pieces):
        produce(0, p, active, share)
    relay(1)
    for p in range(pieces):
        pass_near(0, p)
    collect(1)
    for p in range(pieces):
        pass_head(0, p)
    active, share = expert_set(1)
    for p in range(pieces):
        produce(1, p, active, share)
        pass_depth(0, p)
    for p in range(pieces):
        finish(0, p)
    sent = along[0] + along[1] + across[0] + across[1] + to_depth + to_head
    sent = sent + to_near[0] + to_near[1] + to_core[0] + to_core[1] + core_sums[0] + near_sums[0]

    def settle(p):
        share_of = -(-len(sent) // pieces)
        for copy in sent[p * share_of : (p + 1) * share_of]:
            copy.wait_send()

    steps = (pass_near, pass_head, pass_depth, finish)
    for turn in range(pieces + len(steps) - 1):
        for lag, step in enumerate(steps):
            if 0 <= turn - lag < pieces:
                step(1, turn - lag)
                if step is pass_near:
                    settle(turn - lag)
    sent_same()
    sent_other()
    rest = core_sums[1] + near_sums[1] + head_sums
    for group in depth_sums:
        rest = rest + group
    for copy in rest:
        copy.wait_send()


def fused_layer(
    queries,
    new_keys,
    new_values,
    lengths,
    cache_keys,
    cache_values,
    hidden,
    norm_gain,
    expert_ids,
    gate_levels,
    out_proj,
    gate_w,
    up_w,
    down_w,
):
    pieces = 4
    tokens, width = hidden.shape
    half = width // 2
    rows, heads, head_dim = queries.shape
    inner = heads * head_dim
    cached = cache_keys.shape[1] * cache_keys.shape[2]
    col_width = out_proj.shape[1]
    dev_count = lax.axis_size("dev")
    hidden_units = gate_w.shape[1]
    span = half // pieces
    bf16 = jnp.bfloat16
    vmem = pl.BlockSpec(memory_space=pltpu.VMEM)
    scalars = pl.BlockSpec(memory_space=pltpu.SMEM)
    anywhere = pl.BlockSpec(memory_space=pl.ANY)
    sems = pltpu.SemaphoreType.DMA
    out = pl.pallas_call(
        functools.partial(layer_kernel, pieces),
        out_shape=jax.ShapeDtypeStruct((tokens, width), jnp.float32),
        in_specs=[vmem] * 3 + [scalars] + [anywhere] * 2 + [vmem] * 4 + [anywhere] * 4,
        out_specs=vmem,
        scratch_shapes=[
            pltpu.VMEM((rows, cached, head_dim), bf16),
            pltpu.VMEM((rows, cached, head_dim), bf16),
            pltpu.VMEM((rows * heads, head_dim), jnp.float32),
            pltpu.VMEM((2, dev_count, rows, inner // 2), bf16),
            pltpu.VMEM((2, dev_count // 2, rows, inner // 2), bf16),
            pltpu.VMEM((2, dev_count // 2, rows, inner // 2), bf16),
            pltpu.VMEM(out_proj.shape, bf16),
            pltpu.VMEM((width, hidden_units), bf16),
            pltpu.VMEM((width, hidden_units), bf16),
            pltpu.VMEM((hidden_units, width), bf16),
            pltpu.VMEM((2, dev_count, 2 * tokens, col_width // 2), bf16),
            pltpu.VMEM((2 * dev_count, 2 * tokens, col_width // 2), bf16),
            pltpu.VMEM((tokens, width), jnp.float32),
            pltpu.VMEM((4 * dev_count, 2 * tokens, half + 128), bf16),
            pltpu.VMEM((2 * dev_count, 2 * tokens, half), bf16),
            pltpu.VMEM((2 * dev_count, 2 * tokens, half), bf16),
            pltpu.VMEM((2, pieces, 2, dev_count, 2 * tokens, span), bf16),
            pltpu.VMEM((2, pieces, dev_count, 2 * tokens, span), bf16),
            pltpu.VMEM((2, pieces, dev_count // 2, 2 * tokens, span), bf16),
            pltpu.VMEM((2, pieces, dev_count // 2, 2 * tokens, span), bf16),
            pltpu.VMEM((pieces, dev_count // 2, 2 * tokens, span), bf16),
            pltpu.VMEM((pieces, dev_count // 2, 2 * tokens, span), bf16),
            pltpu.VMEM((pieces, 3, 2 * tokens, span), bf16),
            pltpu.VMEM((pieces, 3, 2 * tokens, span), bf16),
            sems((6,)),
            sems((14,)),
            sems((14,)),
            sems((2 * dev_count - 1,)),
            sems((2 * dev_count - 1,)),
            sems((19,)),
            sems((19,)),
            sems((8 * pieces,)),
            sems((8 * pieces,)),
        ],
        compiler_params=pltpu.CompilerParams(
            collective_id=0, has_side_effects=True, vmem_limit_bytes=56 * 1024 * 1024
        ),
        cost_estimate=pl.CostEstimate(
            flops=3 * 2 * 256 * width * hidden_units, bytes_accessed=16 << 20, transcendentals=0
        ),
    )(
        queries,
        new_keys.reshape(2 * rows, head_dim),
        new_values.reshape(2 * rows, head_dim),
        lengths,
        cache_keys.reshape(rows, cached, head_dim),
        cache_values.reshape(rows, cached, head_dim),
        hidden,
        norm_gain.reshape(1, width),
        expert_ids,
        gate_levels,
        out_proj,
        gate_w,
        up_w,
        down_w,
    )
    return out.astype(bf16)


def on_device(
    hidden,
    queries,
    cache_keys,
    cache_values,
    new_keys,
    new_values,
    lengths,
    out_proj,
    norm_gain,
    expert_gate,
    expert_up,
    expert_down,
    expert_ids,
    gate_levels,
):
    sizes = tuple(lax.axis_size(name) for name in ("role", "dev", "head"))
    if sizes == (2, 8, 2) and hidden.shape[0] == 8 and queries.shape[0] == 16:
        return fused_layer(
            queries,
            new_keys,
            new_values,
            lengths,
            cache_keys,
            cache_values,
            hidden,
            norm_gain,
            expert_ids,
            gate_levels,
            out_proj,
            expert_gate[0],
            expert_up[0],
            expert_down[0],
        )
    attended = attend_block(queries, cache_keys, cache_values, new_keys, new_values, lengths)
    columns = jnp.dot(
        lax.all_gather(attended, "dev", axis=0, tiled=True),
        out_proj,
        preferred_element_type=jnp.float32,
    )
    dev_count = lax.axis_size("dev")
    head_count = lax.axis_size("head")
    experts = lax.axis_size("role") * dev_count
    col_width = out_proj.shape[1]
    width = dev_count * col_width
    projected = lax.all_to_all(columns, ("dev", "head"), split_axis=0, concat_axis=1, tiled=True)
    tokens = projected.shape[0]
    summed = jnp.sum(projected.reshape(tokens, dev_count, head_count, col_width), axis=2).reshape(
        tokens, width
    )
    residual = hidden.astype(jnp.float32) + summed
    normed = (
        residual
        * lax.rsqrt(jnp.mean(residual * residual, axis=-1, keepdims=True) + 1e-06)
        * norm_gain
    ).astype(jnp.bfloat16)
    top_k = expert_ids.shape[1]
    capacity = max(2, 2 * tokens * top_k // experts)
    own_ids = expert_ids.reshape(-1)
    own_ranks = slot_ranks(own_ids, experts)
    pair_rows, pair_ids = (
        lax.all_gather(normed, "head", axis=0, tiled=True),
        lax.all_gather(expert_ids, "head", axis=0, tiled=True),
    )
    pair_flat = pair_ids.reshape(head_count, tokens * top_k)
    pair_ranks = jax.vmap(lambda id_row: slot_ranks(id_row, experts))(pair_flat)
    pair_ranks = pair_ranks + capacity * jnp.arange(head_count, dtype=jnp.int32)[:, None]
    rows_from = jnp.arange(head_count * tokens * top_k, dtype=jnp.int32) // top_k
    outgoing = (
        jnp.zeros((experts, head_count * capacity, width), jnp.bfloat16)
        .at[pair_flat.reshape(-1), pair_ranks.reshape(-1)]
        .set(pair_rows[rows_from])
    )
    incoming = lax.all_to_all(outgoing, ("role", "dev"), split_axis=0, concat_axis=0, tiled=True)
    sources = incoming.shape[0]
    slot_total = incoming.shape[1]
    partial_value = expert_rows(
        incoming.reshape(sources * slot_total, width), expert_gate[0], expert_up[0], expert_down[0]
    )
    partial_value = partial_value.reshape(sources, slot_total, width).astype(jnp.bfloat16)
    arrived = lax.all_to_all(
        partial_value, ("role", "dev"), split_axis=0, concat_axis=0, tiled=True
    )
    arrived = (
        lax.psum_scatter(arrived, "head", scatter_dimension=1, tiled=True)
        .astype(jnp.float32)
        .astype(jnp.bfloat16)
    )
    picked = arrived[own_ids, own_ranks].astype(jnp.float32).reshape(tokens, top_k, width)
    levels = gate_levels.astype(jnp.float32)
    shares = levels / jnp.sum(levels, axis=1, keepdims=True)
    return (residual + jnp.sum(shares[..., None] * picked, axis=1)).astype(jnp.bfloat16)


def solution(mesh):
    placed = (
        P(("role", "dev", "head"), None),
        P(("role", "dev"), "head", None),
        P(("role", "dev"), None, "head", None),
        P(("role", "dev"), None, "head", None),
        P(("role", "dev"), "head", None),
        P(("role", "dev"), "head", None),
        P(("role", "dev")),
        P("head", "dev"),
        P(),
        P(("role", "dev"), None, "head"),
        P(("role", "dev"), None, "head"),
        P(("role", "dev"), "head", None),
        P(("role", "dev", "head"), None),
        P(("role", "dev", "head"), None),
    )
    return jax.shard_map(
        on_device,
        mesh=mesh,
        in_specs=placed,
        out_specs=P(("role", "dev", "head"), None),
        check_vma=False,
    )
```

```python
import functools
import math

import jax
import jax.numpy as jnp
from jax import lax
from jax.experimental import pallas as pl
from jax.experimental.pallas import tpu as pltpu
from jax.sharding import PartitionSpec as P

MESH = pl.DeviceIdType.MESH


def attend_block(query_rows, key_rows, value_rows, key_new, value_new, valid_len):
    row_count = query_rows.shape[0]
    kv_heads = key_rows.shape[2]
    group_size = query_rows.shape[1] // kv_heads
    head_dim = query_rows.shape[2]
    scaling = 1.0 / math.sqrt(head_dim)
    query_f = query_rows.astype(jnp.float32).reshape(row_count, kv_heads, group_size, head_dim)
    scores = jnp.einsum("bhgd,bthd->bhgt", query_f, key_rows.astype(jnp.float32)) * scaling
    scores_new = jnp.einsum("bhgd,bhd->bhg", query_f, key_new.astype(jnp.float32)) * scaling
    positions = jnp.arange(key_rows.shape[1], dtype=jnp.int32)
    usable = (positions[None, :] < valid_len[:, None])[:, None, None, :]
    masked = jnp.where(usable, scores, -1e30)
    highest = jnp.maximum(jnp.max(masked, axis=-1), scores_new)
    exp_terms = jnp.exp(masked - highest[..., None])
    exp_new = jnp.exp(scores_new - highest)
    totals = jnp.sum(exp_terms, axis=-1) + exp_new
    weights = (exp_terms / totals[..., None]).astype(jnp.bfloat16)
    weight_new = (exp_new / totals).astype(jnp.bfloat16)
    blended = jnp.einsum("bhgt,bthd->bhgd", weights, value_rows, preferred_element_type=jnp.float32)
    blended = (
        blended
        + weight_new.astype(jnp.float32)[..., None] * value_new.astype(jnp.float32)[:, :, None, :]
    )
    return blended.astype(jnp.bfloat16).reshape(row_count, kv_heads * group_size * head_dim)


def expert_rows(rows_in, gate_w, up_w, down_w):
    gate_part = jnp.dot(rows_in, gate_w, preferred_element_type=jnp.float32)
    up_part = jnp.dot(rows_in, up_w, preferred_element_type=jnp.float32)
    active = (jax.nn.silu(gate_part) * up_part).astype(jnp.bfloat16)
    return jnp.dot(active, down_w, preferred_element_type=jnp.float32)


def slot_ranks(flat_ids, experts):
    one_hot = (flat_ids[:, None] == jnp.arange(experts, dtype=jnp.int32)[None, :]).astype(jnp.int32)
    return jnp.sum(jnp.cumsum(one_hot, axis=0) * one_hot, axis=1) - 1


def place_of(role, first, second, depth):
    head = first * (1 - role) + second * role
    low = second * (1 - role) + first * role
    return (role, 2 * depth + low, head)


def partner_depths(depth):
    return (depth, depth + 1 - 2 * (depth % 2), depth + 2 - 4 * (depth // 2), 3 - depth)


def layer_kernel(
    pieces,
    query_ref,
    new_key_ref,
    new_value_ref,
    length_ref,
    keys_hbm,
    values_hbm,
    hidden_ref,
    gain_ref,
    ids_ref,
    levels_ref,
    proj_hbm,
    gate_hbm,
    up_hbm,
    down_hbm,
    out_ref,
    keys_ref,
    values_ref,
    att_ref,
    gathered,
    att_low,
    att_high,
    proj_ref,
    gate_ref,
    up_ref,
    down_ref,
    col_out,
    col_in,
    residual_ref,
    token_ref,
    low_ref,
    high_ref,
    active_ref,
    part_ref,
    core_in,
    first_out,
    first_in,
    second_out,
    second_in,
    depth_out,
    depth_in,
    weight_sems,
    att_send,
    att_recv,
    col_send,
    col_recv,
    tok_send,
    tok_recv,
    sum_send,
    sum_recv,
):
    role, dev, head = lax.axis_index("role"), lax.axis_index("dev"), lax.axis_index("head")
    group_count = gathered.shape[1]
    tokens = residual_ref.shape[0]
    width = residual_ref.shape[1]
    half = width // 2
    member = dev * 2 + head
    members = group_count * 2
    low, depth = dev % 2, dev // 2
    first = head * (1 - role) + low * role
    second = low * (1 - role) + head * role
    depths = partner_depths(depth)
    other_core = (1 - role, dev, head)

    loads = [
        pltpu.make_async_copy(source, target, weight_sems.at[number])
        for number, (source, target) in enumerate(
            (
                (proj_hbm, proj_ref),
                (gate_hbm, gate_ref),
                (up_hbm, up_ref),
                (down_hbm, down_ref),
                (keys_hbm, keys_ref),
                (values_hbm, values_ref),
            )
        )
    ]
    for load in loads[4:] + loads[:4]:
        load.start()

    barrier = pltpu.get_barrier_semaphore()

    def greet(step, carry):
        target = (member + step) % members
        pl.semaphore_signal(
            barrier, inc=1, device_id=(role, target // 2, target % 2), device_id_type=MESH
        )
        return carry

    lax.fori_loop(1, members, greet, 0)
    pl.semaphore_signal(barrier, inc=1, device_id=other_core, device_id_type=MESH)

    heads, head_dim = query_ref.shape[1:]
    slots = keys_ref.shape[1]
    shared = heads // 2
    scaling = 1.0 / math.sqrt(head_dim)
    column = lax.broadcasted_iota(jnp.int32, (heads, slots), 1)
    same_head = column % 2 == lax.broadcasted_iota(jnp.int32, (heads, slots), 0) // shared
    new_keys = new_key_ref[...].astype(jnp.float32)
    new_values = new_value_ref[...].astype(jnp.float32)

    def both_heads(rows, request):
        return jnp.concatenate(
            [
                jnp.broadcast_to(rows[2 * request + kv : 2 * request + kv + 1], (shared, head_dim))
                for kv in range(2)
            ],
            axis=0,
        )

    def attend(request):
        query = query_ref[request]
        scores = lax.dot_general(
            query,
            keys_ref[request],
            (((1,), (1,)), ((), ())),
            preferred_element_type=jnp.float32,
        )
        score_new = scaling * jnp.sum(
            query.astype(jnp.float32) * both_heads(new_keys, request), axis=1, keepdims=True
        )
        valid = same_head & (column < 2 * length_ref[request])
        masked = jnp.where(valid, scores * scaling, -1e30)
        highest = jnp.maximum(jnp.max(masked, axis=1, keepdims=True), score_new)
        terms = jnp.exp(masked - highest)
        term_new = jnp.exp(score_new - highest)
        totals = jnp.sum(terms, axis=1, keepdims=True) + term_new
        weights = (terms / totals).astype(jnp.bfloat16)
        weight_new = (term_new / totals).astype(jnp.bfloat16).astype(jnp.float32)
        blended = jnp.dot(weights, values_ref[request], preferred_element_type=jnp.float32)
        att_ref[request * heads : (request + 1) * heads] = blended + weight_new * both_heads(
            new_values, request
        )

    def attend_half(part):
        for request in range(part * tokens, (part + 1) * tokens):
            attend(request)
        for j in range(shared):
            pair = [
                att_ref[pl.ds(part * tokens * heads + kv * shared + j, tokens, stride=heads), :]
                for kv in range(2)
            ]
            gathered[part, dev, :, j * head_dim : (j + 1) * head_dim] = jnp.concatenate(
                pair, axis=0
            ).astype(jnp.bfloat16)

    def att_copy(part, depth_from, target, number):
        block = gathered.at[part, 2 * depth_from + low]
        return pltpu.make_async_remote_copy(
            src_ref=block,
            dst_ref=block,
            send_sem=att_send.at[7 * part + number],
            recv_sem=att_recv.at[7 * part + number],
            device_id=target,
            device_id_type=MESH,
        )

    beside = (role, 2 * depth + 1 - low, head)
    along = [
        [att_copy(part, depth, (role, 2 * depths[k] + low, head), k - 1) for k in (1, 2, 3)]
        for part in range(2)
    ]
    across = [
        [att_copy(part, depths[k], beside, 3 + k) for k in range(4)] for part in range(2)
    ]
    loads[4].wait()
    loads[5].wait()
    for part in range(2):
        attend_half(part)
        if part == 0:
            pl.semaphore_wait(barrier, members)
        across[part][0].start()
        for copy in along[part]:
            copy.start()

    def unfold_att(block):
        one = gathered[0, block].astype(jnp.float32)
        two = gathered[1, block].astype(jnp.float32)
        att_low[block] = jnp.concatenate([one[:tokens], two[:tokens]], axis=0).astype(jnp.bfloat16)
        att_high[block] = jnp.concatenate([one[tokens:], two[tokens:]], axis=0).astype(
            jnp.bfloat16
        )

    for part in range(2):
        for k in (1, 2, 3):
            along[part][k - 1].wait_recv()
            across[part][k].start()
    for k in range(4):
        unfold_att(2 * depths[k] + low)
    for k in range(4):
        across[0][k].wait_recv()
    for k in range(4):
        across[1][k].wait_recv()
        unfold_att(2 * depths[k] + 1 - low)

    loads[0].wait()
    fold = att_low.shape[2]
    rows = group_count * 2 * tokens
    columns = jnp.dot(
        att_low[...].reshape(rows, fold), proj_ref[:fold], preferred_element_type=jnp.float32
    ) + jnp.dot(
        att_high[...].reshape(rows, fold), proj_ref[fold:], preferred_element_type=jnp.float32
    )
    col_width = columns.shape[1]
    columns = columns.reshape(members, tokens, col_width)
    col_out[...] = jnp.concatenate(
        [columns[:, :, : col_width // 2], columns[:, :, col_width // 2 :]], axis=1
    ).astype(jnp.bfloat16)

    def col_copy(step):
        target = (member + step) % members
        return pltpu.make_async_remote_copy(
            src_ref=col_out.at[target],
            dst_ref=col_in.at[member],
            send_sem=col_send.at[step - 1],
            recv_sem=col_recv.at[step - 1],
            device_id=(role, target // 2, target % 2),
            device_id_type=MESH,
        )

    def col_start(step, carry):
        col_copy(step).start()
        return carry

    def col_sent(step, carry):
        col_copy(step).wait_send()
        return carry

    def col_arrive(step, carry):
        col_copy(step).wait_recv()
        return carry

    lax.fori_loop(1, members, col_start, 0)
    col_in[member] = col_out[member]
    lanes = lax.broadcasted_iota(jnp.int32, (tokens, 128), 1)
    named = jnp.zeros((tokens, 128), jnp.float32)
    for k in range(ids_ref.shape[1]):
        level = levels_ref[:, k : k + 1].astype(jnp.float32)
        named = named + jnp.where(lanes == ids_ref[:, k : k + 1], level, 0.0)
    slot = role * 16 + first * 8 + second * 4 + depth
    token_ref[slot, :, half:] = jnp.concatenate(
        [named, jnp.zeros((tokens, 128), jnp.float32)], axis=0
    ).astype(jnp.bfloat16)
    lax.fori_loop(1, members, col_arrive, 0)

    for block in range(group_count):
        both = col_in[2 * block].astype(jnp.float32) + col_in[2 * block + 1].astype(jnp.float32)
        for side in range(2):
            edge = block * col_width + side * (col_width // 2)
            span = slice(edge, edge + col_width // 2)
            residual_ref[:, span] = (
                hidden_ref[:, span].astype(jnp.float32) + both[side * tokens : (side + 1) * tokens]
            )
    residual = residual_ref[...]
    square = jnp.sum(residual * residual, axis=-1, keepdims=True) / width
    normed = residual * lax.rsqrt(square + 1e-06) * gain_ref[...]
    token_ref[slot, :, :half] = jnp.concatenate(
        [normed[:, :half], normed[:, half:]], axis=0
    ).astype(jnp.bfloat16)

    def token_copy(start, count, target, number):
        block = token_ref.at[pl.ds(start, count)]
        return pltpu.make_async_remote_copy(
            src_ref=block,
            dst_ref=block,
            send_sem=tok_send.at[number],
            recv_sem=tok_recv.at[number],
            device_id=target,
            device_id_type=MESH,
        )

    def slot_of(first_at, second_at, depth_at):
        return role * 16 + first_at * 8 + second_at * 4 + depth_at

    second_side = place_of(role, first, 1 - second, depth)
    first_side = place_of(role, 1 - first, second, depth)
    own = [slot_of(first, second, depths[k]) for k in range(4)]
    near = [slot_of(first, 1 - second, depths[k]) for k in range(4)]
    to_depth = [
        token_copy(own[0], 1, place_of(role, first, second, depths[k]), k - 1) for k in (1, 2, 3)
    ]
    to_second = [token_copy(own[k], 1, second_side, 3 + k) for k in range(4)]
    to_first = [token_copy(own[k], 1, first_side, 7 + k) for k in range(4)]
    to_first = to_first + [token_copy(near[k], 1, first_side, 11 + k) for k in range(4)]
    to_core = [
        token_copy(slot_of(*corner, 0), 4, other_core, 15 + number)
        for number, corner in enumerate(
            ((first, second), (first, 1 - second), (1 - first, second), (1 - first, 1 - second))
        )
    ]
    to_second[0].start()
    to_first[0].start()
    for copy in to_depth:
        copy.start()
    for k in range(4):
        if k > 0:
            to_depth[k - 1].wait_recv()
            to_second[k].start()
            to_first[k].start()
            if k == 3:
                to_core[0].start()
        if k < 3:
            to_second[k].wait_recv()
            to_first[4 + k].start()

    def unfold(pair, carry):
        one = token_ref[2 * pair, :, :half].astype(jnp.float32)
        two = token_ref[2 * pair + 1, :, :half].astype(jnp.float32)
        low_ref[pair] = jnp.concatenate([one[:tokens], two[:tokens]], axis=0).astype(jnp.bfloat16)
        high_ref[pair] = jnp.concatenate([one[tokens:], two[tokens:]], axis=0).astype(jnp.bfloat16)
        return carry

    def unfold_from(role_at, first_at, second_at):
        start = role_at * 8 + first_at * 4 + second_at * 2
        lax.fori_loop(start, start + 2, unfold, 0)

    pairs = low_ref.shape[0]
    total_rows = pairs * 2 * tokens
    set_rows = total_rows // 4
    set_pairs = pairs // 4

    def expert_set(first_own, first_other):
        sides = []
        for ref in (low_ref, high_ref):
            both = [
                ref[pl.ds(role * 8 + first_own * 4, set_pairs)],
                ref[pl.ds((1 - role) * 8 + first_other * 4, set_pairs)],
            ]
            sides.append(jnp.concatenate(both, axis=0).reshape(2 * set_rows, half))

        def through(weight_ref):
            return jnp.dot(
                sides[0], weight_ref[:half], preferred_element_type=jnp.float32
            ) + jnp.dot(sides[1], weight_ref[half:], preferred_element_type=jnp.float32)

        gate_part = through(gate_ref)
        up_part = through(up_ref)
        active = (gate_part / (1.0 + jnp.exp(-gate_part)) * up_part).astype(jnp.bfloat16)
        active_ref[role * 2 + first_own] = active[:set_rows]
        active_ref[(1 - role) * 2 + first_other] = active[set_rows:]

    unfold_from(role, first, second)
    to_second[3].wait_recv()
    to_first[7].start()
    to_core[1].start()
    unfold_from(role, first, 1 - second)
    lax.fori_loop(1, members, col_sent, 0)
    for part in range(2):
        for copy in along[part] + across[part]:
            copy.wait_send()
    for load in loads[1:4]:
        load.wait()
    for k in range(4):
        to_first[k].wait_recv()
    to_core[2].start()
    to_core[0].wait_recv()
    unfold_from(1 - role, second, first)
    to_core[1].wait_recv()
    unfold_from(1 - role, second, 1 - first)
    unfold_from(role, 1 - first, second)
    for k in range(4, 8):
        to_first[k].wait_recv()
    to_core[3].start()
    expert_set(first, second)
    unfold_from(role, 1 - first, 1 - second)
    to_core[2].wait_recv()
    unfold_from(1 - role, 1 - second, first)
    to_core[3].wait_recv()
    unfold_from(1 - role, 1 - second, 1 - first)
    expert_set(1 - first, 1 - second)
    table = token_ref[:, :, half:].astype(jnp.float32)[:, :tokens].reshape(total_rows, 128)
    mine = lax.broadcasted_iota(jnp.int32, (total_rows, 128), 1) == role * group_count + dev
    share = jnp.sum(jnp.where(mine, table, 0.0), axis=1, keepdims=True) / jnp.sum(
        table, axis=1, keepdims=True
    )

    span_width = half // pieces

    def sum_copy(source, target, device, number):
        return pltpu.make_async_remote_copy(
            src_ref=source,
            dst_ref=target,
            send_sem=sum_send.at[number],
            recv_sem=sum_recv.at[number],
            device_id=device,
            device_id_type=MESH,
        )

    core_sums = [
        sum_copy(part_ref.at[p, pl.ds((1 - role) * 16, 16)], core_in.at[p], other_core, 6 * p)
        for p in range(pieces)
    ]
    first_sums = [
        sum_copy(first_out.at[p], first_in.at[p], first_side, 6 * p + 1) for p in range(pieces)
    ]
    second_sums = [
        sum_copy(second_out.at[p], second_in.at[p], second_side, 6 * p + 2) for p in range(pieces)
    ]
    depth_sums = [
        [
            sum_copy(
                depth_out.at[p, k - 1],
                depth_in.at[p, k - 1],
                place_of(role, first, second, depths[k]),
                6 * p + 2 + k,
            )
            for k in (1, 2, 3)
        ]
        for p in range(pieces)
    ]

    active_rows = active_ref[...].reshape(total_rows, active_ref.shape[2])

    def produce(p):
        sides = []
        for side in range(2):
            edge = side * half + p * span_width
            product = jnp.dot(
                active_rows, down_ref[:, edge : edge + span_width], preferred_element_type=jnp.float32
            )
            sides.append((product * share).reshape(2 * pairs, tokens, span_width))
        part_ref[p] = jnp.concatenate(sides, axis=1).astype(jnp.bfloat16)
        core_sums[p].start()

    def core_total(p, start, count):
        return part_ref[p, pl.ds(role * 16 + start, count)].astype(jnp.float32) + core_in[
            p, pl.ds(start, count)
        ].astype(jnp.float32)

    def pass_first(p):
        core_sums[p].wait_recv()
        first_out[p] = core_total(p, (1 - first) * 8, 8).astype(jnp.bfloat16)
        first_sums[p].start()

    def first_total(p, second_at, depth_at, count):
        start = second_at * 4 + depth_at
        return core_total(p, first * 8 + start, count) + first_in[p, pl.ds(start, count)].astype(
            jnp.float32
        )

    def pass_second(p):
        first_sums[p].wait_recv()
        second_out[p] = first_total(p, 1 - second, 0, 4).astype(jnp.bfloat16)
        second_sums[p].start()

    def second_total(p, depth_at):
        return first_total(p, second, depth_at, 1)[0] + second_in[p, depth_at].astype(jnp.float32)

    def pass_depth(p):
        second_sums[p].wait_recv()
        for k in (1, 2, 3):
            depth_out[p, k - 1] = second_total(p, depths[k]).astype(jnp.bfloat16)
            depth_sums[p][k - 1].start()

    def finish(p):
        total = second_total(p, depth)
        for k in range(3):
            depth_sums[p][k].wait_recv()
            total = total + depth_in[p, k].astype(jnp.float32)
        for side in range(2):
            edge = side * half + p * span_width
            span = slice(edge, edge + span_width)
            out_ref[:, span] = (
                residual_ref[:, span] + total[side * tokens : (side + 1) * tokens]
            )

    sent = to_depth + to_second + to_first + to_core

    def settle(p):
        share_of = -(-len(sent) // pieces)
        for copy in sent[p * share_of : (p + 1) * share_of]:
            copy.wait_send()
        for copy in (core_sums[p], first_sums[p], second_sums[p]):
            copy.wait_send()

    for p in range(pieces):
        produce(p)
        if p > 1:
            pass_first(p - 2)
    for p in range(max(pieces - 2, 0), pieces):
        pass_first(p)
    for p in range(pieces):
        pass_second(p)
    for p in range(pieces):
        pass_depth(p)
        settle(p)
    for p in range(pieces):
        finish(p)
    for group in depth_sums:
        for copy in group:
            copy.wait_send()


def fused_layer(
    queries,
    new_keys,
    new_values,
    lengths,
    cache_keys,
    cache_values,
    hidden,
    norm_gain,
    expert_ids,
    gate_levels,
    out_proj,
    gate_w,
    up_w,
    down_w,
):
    pieces = 4
    tokens, width = hidden.shape
    half = width // 2
    rows, heads, head_dim = queries.shape
    inner = heads * head_dim
    cached = cache_keys.shape[1] * cache_keys.shape[2]
    col_width = out_proj.shape[1]
    dev_count = lax.axis_size("dev")
    hidden_units = gate_w.shape[1]
    span = half // pieces
    bf16 = jnp.bfloat16
    vmem = pl.BlockSpec(memory_space=pltpu.VMEM)
    scalars = pl.BlockSpec(memory_space=pltpu.SMEM)
    anywhere = pl.BlockSpec(memory_space=pl.ANY)
    sems = pltpu.SemaphoreType.DMA
    out = pl.pallas_call(
        functools.partial(layer_kernel, pieces),
        out_shape=jax.ShapeDtypeStruct((tokens, width), jnp.float32),
        in_specs=[vmem] * 3 + [scalars] + [anywhere] * 2 + [vmem] * 4 + [anywhere] * 4,
        out_specs=vmem,
        scratch_shapes=[
            pltpu.VMEM((rows, cached, head_dim), bf16),
            pltpu.VMEM((rows, cached, head_dim), bf16),
            pltpu.VMEM((rows * heads, head_dim), jnp.float32),
            pltpu.VMEM((2, dev_count, rows, inner // 2), bf16),
            pltpu.VMEM((dev_count, rows, inner // 2), bf16),
            pltpu.VMEM((dev_count, rows, inner // 2), bf16),
            pltpu.VMEM(out_proj.shape, bf16),
            pltpu.VMEM((width, hidden_units), bf16),
            pltpu.VMEM((width, hidden_units), bf16),
            pltpu.VMEM((hidden_units, width), bf16),
            pltpu.VMEM((2 * dev_count, 2 * tokens, col_width // 2), bf16),
            pltpu.VMEM((2 * dev_count, 2 * tokens, col_width // 2), bf16),
            pltpu.VMEM((tokens, width), jnp.float32),
            pltpu.VMEM((4 * dev_count, 2 * tokens, half + 128), bf16),
            pltpu.VMEM((2 * dev_count, 2 * tokens, half), bf16),
            pltpu.VMEM((2 * dev_count, 2 * tokens, half), bf16),
            pltpu.VMEM((4, 8 * tokens, hidden_units), bf16),
            pltpu.VMEM((pieces, 32, 2 * tokens, span), bf16),
            pltpu.VMEM((pieces, 16, 2 * tokens, span), bf16),
            pltpu.VMEM((pieces, 8, 2 * tokens, span), bf16),
            pltpu.VMEM((pieces, 8, 2 * tokens, span), bf16),
            pltpu.VMEM((pieces, 4, 2 * tokens, span), bf16),
            pltpu.VMEM((pieces, 4, 2 * tokens, span), bf16),
            pltpu.VMEM((pieces, 3, 2 * tokens, span), bf16),
            pltpu.VMEM((pieces, 3, 2 * tokens, span), bf16),
            sems((6,)),
            sems((14,)),
            sems((14,)),
            sems((2 * dev_count - 1,)),
            sems((2 * dev_count - 1,)),
            sems((19,)),
            sems((19,)),
            sems((6 * pieces,)),
            sems((6 * pieces,)),
        ],
        compiler_params=pltpu.CompilerParams(
            collective_id=0, has_side_effects=True, vmem_limit_bytes=56 * 1024 * 1024
        ),
        cost_estimate=pl.CostEstimate(
            flops=3 * 2 * 256 * width * hidden_units, bytes_accessed=16 << 20, transcendentals=0
        ),
    )(
        queries,
        new_keys.reshape(2 * rows, head_dim),
        new_values.reshape(2 * rows, head_dim),
        lengths,
        cache_keys.reshape(rows, cached, head_dim),
        cache_values.reshape(rows, cached, head_dim),
        hidden,
        norm_gain.reshape(1, width),
        expert_ids,
        gate_levels,
        out_proj,
        gate_w,
        up_w,
        down_w,
    )
    return out.astype(bf16)


def on_device(
    hidden,
    queries,
    cache_keys,
    cache_values,
    new_keys,
    new_values,
    lengths,
    out_proj,
    norm_gain,
    expert_gate,
    expert_up,
    expert_down,
    expert_ids,
    gate_levels,
):
    sizes = tuple(lax.axis_size(name) for name in ("role", "dev", "head"))
    if sizes == (2, 8, 2) and hidden.shape[0] == 8 and queries.shape[0] == 16:
        return fused_layer(
            queries,
            new_keys,
            new_values,
            lengths,
            cache_keys,
            cache_values,
            hidden,
            norm_gain,
            expert_ids,
            gate_levels,
            out_proj,
            expert_gate[0],
            expert_up[0],
            expert_down[0],
        )
    attended = attend_block(queries, cache_keys, cache_values, new_keys, new_values, lengths)
    columns = jnp.dot(
        lax.all_gather(attended, "dev", axis=0, tiled=True),
        out_proj,
        preferred_element_type=jnp.float32,
    )
    dev_count = lax.axis_size("dev")
    head_count = lax.axis_size("head")
    experts = lax.axis_size("role") * dev_count
    col_width = out_proj.shape[1]
    width = dev_count * col_width
    projected = lax.all_to_all(columns, ("dev", "head"), split_axis=0, concat_axis=1, tiled=True)
    tokens = projected.shape[0]
    summed = jnp.sum(projected.reshape(tokens, dev_count, head_count, col_width), axis=2).reshape(
        tokens, width
    )
    residual = hidden.astype(jnp.float32) + summed
    normed = (
        residual
        * lax.rsqrt(jnp.mean(residual * residual, axis=-1, keepdims=True) + 1e-06)
        * norm_gain
    ).astype(jnp.bfloat16)
    top_k = expert_ids.shape[1]
    capacity = max(2, 2 * tokens * top_k // experts)
    own_ids = expert_ids.reshape(-1)
    own_ranks = slot_ranks(own_ids, experts)
    pair_rows, pair_ids = (
        lax.all_gather(normed, "head", axis=0, tiled=True),
        lax.all_gather(expert_ids, "head", axis=0, tiled=True),
    )
    pair_flat = pair_ids.reshape(head_count, tokens * top_k)
    pair_ranks = jax.vmap(lambda id_row: slot_ranks(id_row, experts))(pair_flat)
    pair_ranks = pair_ranks + capacity * jnp.arange(head_count, dtype=jnp.int32)[:, None]
    rows_from = jnp.arange(head_count * tokens * top_k, dtype=jnp.int32) // top_k
    outgoing = (
        jnp.zeros((experts, head_count * capacity, width), jnp.bfloat16)
        .at[pair_flat.reshape(-1), pair_ranks.reshape(-1)]
        .set(pair_rows[rows_from])
    )
    incoming = lax.all_to_all(outgoing, ("role", "dev"), split_axis=0, concat_axis=0, tiled=True)
    sources = incoming.shape[0]
    slot_total = incoming.shape[1]
    partial_value = expert_rows(
        incoming.reshape(sources * slot_total, width), expert_gate[0], expert_up[0], expert_down[0]
    )
    partial_value = partial_value.reshape(sources, slot_total, width).astype(jnp.bfloat16)
    arrived = lax.all_to_all(
        partial_value, ("role", "dev"), split_axis=0, concat_axis=0, tiled=True
    )
    arrived = (
        lax.psum_scatter(arrived, "head", scatter_dimension=1, tiled=True)
        .astype(jnp.float32)
        .astype(jnp.bfloat16)
    )
    picked = arrived[own_ids, own_ranks].astype(jnp.float32).reshape(tokens, top_k, width)
    levels = gate_levels.astype(jnp.float32)
    shares = levels / jnp.sum(levels, axis=1, keepdims=True)
    return (residual + jnp.sum(shares[..., None] * picked, axis=1)).astype(jnp.bfloat16)


def solution(mesh):
    placed = (
        P(("role", "dev", "head"), None),
        P(("role", "dev"), "head", None),
        P(("role", "dev"), None, "head", None),
        P(("role", "dev"), None, "head", None),
        P(("role", "dev"), "head", None),
        P(("role", "dev"), "head", None),
        P(("role", "dev")),
        P("head", "dev"),
        P(),
        P(("role", "dev"), None, "head"),
        P(("role", "dev"), None, "head"),
        P(("role", "dev"), "head", None),
        P(("role", "dev", "head"), None),
        P(("role", "dev", "head"), None),
    )
    return jax.shard_map(
        on_device,
        mesh=mesh,
        in_specs=placed,
        out_specs=P(("role", "dev", "head"), None),
        check_vma=False,
    )
```

```python
import functools
import math

import jax
import jax.numpy as jnp
from jax import lax
from jax.experimental import pallas as pl
from jax.experimental.pallas import tpu as pltpu
from jax.sharding import PartitionSpec as P

MESH = pl.DeviceIdType.MESH


def attend_block(query_rows, key_rows, value_rows, key_new, value_new, valid_len):
    row_count = query_rows.shape[0]
    kv_heads = key_rows.shape[2]
    group_size = query_rows.shape[1] // kv_heads
    head_dim = query_rows.shape[2]
    scaling = 1.0 / math.sqrt(head_dim)
    query_f = query_rows.astype(jnp.float32).reshape(row_count, kv_heads, group_size, head_dim)
    scores = jnp.einsum("bhgd,bthd->bhgt", query_f, key_rows.astype(jnp.float32)) * scaling
    scores_new = jnp.einsum("bhgd,bhd->bhg", query_f, key_new.astype(jnp.float32)) * scaling
    positions = jnp.arange(key_rows.shape[1], dtype=jnp.int32)
    usable = (positions[None, :] < valid_len[:, None])[:, None, None, :]
    masked = jnp.where(usable, scores, -1e30)
    highest = jnp.maximum(jnp.max(masked, axis=-1), scores_new)
    exp_terms = jnp.exp(masked - highest[..., None])
    exp_new = jnp.exp(scores_new - highest)
    totals = jnp.sum(exp_terms, axis=-1) + exp_new
    weights = (exp_terms / totals[..., None]).astype(jnp.bfloat16)
    weight_new = (exp_new / totals).astype(jnp.bfloat16)
    blended = jnp.einsum("bhgt,bthd->bhgd", weights, value_rows, preferred_element_type=jnp.float32)
    blended = (
        blended
        + weight_new.astype(jnp.float32)[..., None] * value_new.astype(jnp.float32)[:, :, None, :]
    )
    return blended.astype(jnp.bfloat16).reshape(row_count, kv_heads * group_size * head_dim)


def expert_rows(rows_in, gate_w, up_w, down_w):
    gate_part = jnp.dot(rows_in, gate_w, preferred_element_type=jnp.float32)
    up_part = jnp.dot(rows_in, up_w, preferred_element_type=jnp.float32)
    active = (jax.nn.silu(gate_part) * up_part).astype(jnp.bfloat16)
    return jnp.dot(active, down_w, preferred_element_type=jnp.float32)


def slot_ranks(flat_ids, experts):
    one_hot = (flat_ids[:, None] == jnp.arange(experts, dtype=jnp.int32)[None, :]).astype(jnp.int32)
    return jnp.sum(jnp.cumsum(one_hot, axis=0) * one_hot, axis=1) - 1


def place_of(role, first, second, depth):
    head = first * (1 - role) + second * role
    low = second * (1 - role) + first * role
    return (role, 2 * depth + low, head)


def partner_depths(depth):
    return (depth, depth + 1 - 2 * (depth % 2), depth + 2 - 4 * (depth // 2), 3 - depth)


def layer_kernel(
    pieces,
    query_ref,
    new_key_ref,
    new_value_ref,
    length_ref,
    keys_hbm,
    values_hbm,
    hidden_ref,
    gain_ref,
    ids_ref,
    levels_ref,
    proj_hbm,
    gate_hbm,
    up_hbm,
    down_hbm,
    out_ref,
    keys_ref,
    values_ref,
    att_ref,
    gathered,
    att_low,
    att_high,
    proj_ref,
    gate_ref,
    up_ref,
    down_ref,
    col_out,
    col_in,
    residual_ref,
    token_ref,
    low_ref,
    high_ref,
    part_ref,
    core_in,
    first_out,
    first_in,
    second_out,
    second_in,
    depth_out,
    depth_in,
    weight_sems,
    att_send,
    att_recv,
    col_send,
    col_recv,
    tok_send,
    tok_recv,
    sum_send,
    sum_recv,
):
    role, dev, head = lax.axis_index("role"), lax.axis_index("dev"), lax.axis_index("head")
    group_count = gathered.shape[1]
    tokens = residual_ref.shape[0]
    width = residual_ref.shape[1]
    half = width // 2
    member = dev * 2 + head
    members = group_count * 2
    low, depth = dev % 2, dev // 2
    first = head * (1 - role) + low * role
    second = low * (1 - role) + head * role
    depths = partner_depths(depth)
    other_core = (1 - role, dev, head)

    loads = [
        pltpu.make_async_copy(source, target, weight_sems.at[number])
        for number, (source, target) in enumerate(
            (
                (proj_hbm, proj_ref),
                (gate_hbm, gate_ref),
                (up_hbm, up_ref),
                (down_hbm, down_ref),
                (keys_hbm, keys_ref),
                (values_hbm, values_ref),
            )
        )
    ]
    for load in loads[4:] + loads[:4]:
        load.start()

    barrier = pltpu.get_barrier_semaphore()

    def greet(step, carry):
        target = (member + step) % members
        pl.semaphore_signal(
            barrier, inc=1, device_id=(role, target // 2, target % 2), device_id_type=MESH
        )
        return carry

    lax.fori_loop(1, members, greet, 0)
    pl.semaphore_signal(barrier, inc=1, device_id=other_core, device_id_type=MESH)

    heads, head_dim = query_ref.shape[1:]
    slots = keys_ref.shape[1]
    shared = heads // 2
    scaling = 1.0 / math.sqrt(head_dim)
    column = lax.broadcasted_iota(jnp.int32, (heads, slots), 1)
    same_head = column % 2 == lax.broadcasted_iota(jnp.int32, (heads, slots), 0) // shared
    new_keys = new_key_ref[...].astype(jnp.float32)
    new_values = new_value_ref[...].astype(jnp.float32)

    def both_heads(rows, request):
        return jnp.concatenate(
            [
                jnp.broadcast_to(rows[2 * request + kv : 2 * request + kv + 1], (shared, head_dim))
                for kv in range(2)
            ],
            axis=0,
        )

    def attend(request):
        query = query_ref[request]
        scores = lax.dot_general(
            query,
            keys_ref[request],
            (((1,), (1,)), ((), ())),
            preferred_element_type=jnp.float32,
        )
        score_new = scaling * jnp.sum(
            query.astype(jnp.float32) * both_heads(new_keys, request), axis=1, keepdims=True
        )
        valid = same_head & (column < 2 * length_ref[request])
        masked = jnp.where(valid, scores * scaling, -1e30)
        highest = jnp.maximum(jnp.max(masked, axis=1, keepdims=True), score_new)
        terms = jnp.exp(masked - highest)
        term_new = jnp.exp(score_new - highest)
        totals = jnp.sum(terms, axis=1, keepdims=True) + term_new
        weights = (terms / totals).astype(jnp.bfloat16)
        weight_new = (term_new / totals).astype(jnp.bfloat16).astype(jnp.float32)
        blended = jnp.dot(weights, values_ref[request], preferred_element_type=jnp.float32)
        att_ref[request * heads : (request + 1) * heads] = blended + weight_new * both_heads(
            new_values, request
        )

    def attend_half(part):
        for request in range(part * tokens, (part + 1) * tokens):
            attend(request)
        for j in range(shared):
            pair = [
                att_ref[pl.ds(part * tokens * heads + kv * shared + j, tokens, stride=heads), :]
                for kv in range(2)
            ]
            gathered[part, dev, :, j * head_dim : (j + 1) * head_dim] = jnp.concatenate(
                pair, axis=0
            ).astype(jnp.bfloat16)

    def att_copy(part, depth_from, target, number):
        block = gathered.at[part, 2 * depth_from + low]
        return pltpu.make_async_remote_copy(
            src_ref=block,
            dst_ref=block,
            send_sem=att_send.at[7 * part + number],
            recv_sem=att_recv.at[7 * part + number],
            device_id=target,
            device_id_type=MESH,
        )

    beside = (role, 2 * depth + 1 - low, head)
    along = [
        [att_copy(part, depth, (role, 2 * depths[k] + low, head), k - 1) for k in (1, 2, 3)]
        for part in range(2)
    ]
    across = [
        [att_copy(part, depths[k], beside, 3 + k) for k in range(4)] for part in range(2)
    ]
    loads[4].wait()
    loads[5].wait()
    for part in range(2):
        attend_half(part)
        if part == 0:
            pl.semaphore_wait(barrier, members)
        across[part][0].start()
        for copy in along[part]:
            copy.start()

    def unfold_att(block):
        one = gathered[0, block].astype(jnp.float32)
        two = gathered[1, block].astype(jnp.float32)
        att_low[block] = jnp.concatenate([one[:tokens], two[:tokens]], axis=0).astype(jnp.bfloat16)
        att_high[block] = jnp.concatenate([one[tokens:], two[tokens:]], axis=0).astype(
            jnp.bfloat16
        )

    for part in range(2):
        for k in (1, 2, 3):
            along[part][k - 1].wait_recv()
            across[part][k].start()
    for k in range(4):
        unfold_att(2 * depths[k] + low)
    for k in range(4):
        across[0][k].wait_recv()
    for k in range(4):
        across[1][k].wait_recv()
        unfold_att(2 * depths[k] + 1 - low)

    loads[0].wait()
    fold = att_low.shape[2]
    rows = group_count * 2 * tokens
    columns = jnp.dot(
        att_low[...].reshape(rows, fold), proj_ref[:fold], preferred_element_type=jnp.float32
    ) + jnp.dot(
        att_high[...].reshape(rows, fold), proj_ref[fold:], preferred_element_type=jnp.float32
    )
    col_width = columns.shape[1]
    columns = columns.reshape(members, tokens, col_width)
    col_out[...] = jnp.concatenate(
        [columns[:, :, : col_width // 2], columns[:, :, col_width // 2 :]], axis=1
    ).astype(jnp.bfloat16)

    def col_copy(step):
        target = (member + step) % members
        return pltpu.make_async_remote_copy(
            src_ref=col_out.at[target],
            dst_ref=col_in.at[member],
            send_sem=col_send.at[step - 1],
            recv_sem=col_recv.at[step - 1],
            device_id=(role, target // 2, target % 2),
            device_id_type=MESH,
        )

    def col_start(step, carry):
        col_copy(step).start()
        return carry

    def col_sent(step, carry):
        col_copy(step).wait_send()
        return carry

    def col_arrive(step, carry):
        col_copy(step).wait_recv()
        return carry

    lax.fori_loop(1, members, col_start, 0)
    col_in[member] = col_out[member]
    lanes = lax.broadcasted_iota(jnp.int32, (tokens, 128), 1)
    named = jnp.zeros((tokens, 128), jnp.float32)
    for k in range(ids_ref.shape[1]):
        level = levels_ref[:, k : k + 1].astype(jnp.float32)
        named = named + jnp.where(lanes == ids_ref[:, k : k + 1], level, 0.0)
    slot = role * 16 + first * 8 + second * 4 + depth
    token_ref[slot, :, half:] = jnp.concatenate(
        [named, jnp.zeros((tokens, 128), jnp.float32)], axis=0
    ).astype(jnp.bfloat16)
    lax.fori_loop(1, members, col_arrive, 0)

    for block in range(group_count):
        both = col_in[2 * block].astype(jnp.float32) + col_in[2 * block + 1].astype(jnp.float32)
        for side in range(2):
            edge = block * col_width + side * (col_width // 2)
            span = slice(edge, edge + col_width // 2)
            residual_ref[:, span] = (
                hidden_ref[:, span].astype(jnp.float32) + both[side * tokens : (side + 1) * tokens]
            )
    residual = residual_ref[...]
    square = jnp.sum(residual * residual, axis=-1, keepdims=True) / width
    normed = residual * lax.rsqrt(square + 1e-06) * gain_ref[...]
    token_ref[slot, :, :half] = jnp.concatenate(
        [normed[:, :half], normed[:, half:]], axis=0
    ).astype(jnp.bfloat16)

    def token_copy(start, count, target, number):
        block = token_ref.at[pl.ds(start, count)]
        return pltpu.make_async_remote_copy(
            src_ref=block,
            dst_ref=block,
            send_sem=tok_send.at[number],
            recv_sem=tok_recv.at[number],
            device_id=target,
            device_id_type=MESH,
        )

    def slot_of(first_at, second_at, depth_at):
        return role * 16 + first_at * 8 + second_at * 4 + depth_at

    second_side = place_of(role, first, 1 - second, depth)
    first_side = place_of(role, 1 - first, second, depth)
    own = [slot_of(first, second, depths[k]) for k in range(4)]
    near = [slot_of(first, 1 - second, depths[k]) for k in range(4)]
    to_depth = [
        token_copy(own[0], 1, place_of(role, first, second, depths[k]), k - 1) for k in (1, 2, 3)
    ]
    to_second = [token_copy(own[k], 1, second_side, 3 + k) for k in range(4)]
    to_first = [token_copy(own[k], 1, first_side, 7 + k) for k in range(4)]
    to_first = to_first + [token_copy(near[k], 1, first_side, 11 + k) for k in range(4)]
    to_core = [
        token_copy(slot_of(*corner, 0), 4, other_core, 15 + number)
        for number, corner in enumerate(
            ((first, second), (first, 1 - second), (1 - first, second), (1 - first, 1 - second))
        )
    ]
    to_second[0].start()
    to_first[0].start()
    for copy in to_depth:
        copy.start()
    for k in range(4):
        if k > 0:
            to_depth[k - 1].wait_recv()
            to_second[k].start()
            to_first[k].start()
            if k == 3:
                to_core[0].start()
        if k < 3:
            to_second[k].wait_recv()
            to_first[4 + k].start()

    def unfold(pair, carry):
        one = token_ref[2 * pair, :, :half].astype(jnp.float32)
        two = token_ref[2 * pair + 1, :, :half].astype(jnp.float32)
        low_ref[pair] = jnp.concatenate([one[:tokens], two[:tokens]], axis=0).astype(jnp.bfloat16)
        high_ref[pair] = jnp.concatenate([one[tokens:], two[tokens:]], axis=0).astype(jnp.bfloat16)
        return carry

    def unfold_from(role_at, first_at, second_at):
        start = role_at * 8 + first_at * 4 + second_at * 2
        lax.fori_loop(start, start + 2, unfold, 0)

    pairs = low_ref.shape[0]
    total_rows = pairs * 2 * tokens
    unfold_from(role, first, second)
    to_second[3].wait_recv()
    to_first[7].start()
    to_core[1].start()
    unfold_from(role, first, 1 - second)
    lax.fori_loop(1, members, col_sent, 0)
    for part in range(2):
        for copy in along[part] + across[part]:
            copy.wait_send()
    for load in loads[1:4]:
        load.wait()
    for k in range(4):
        to_first[k].wait_recv()
    to_core[2].start()
    to_core[0].wait_recv()
    unfold_from(1 - role, second, first)
    to_core[1].wait_recv()
    unfold_from(1 - role, second, 1 - first)
    unfold_from(role, 1 - first, second)
    for k in range(4, 8):
        to_first[k].wait_recv()
    to_core[3].start()
    unfold_from(role, 1 - first, 1 - second)
    to_core[2].wait_recv()
    unfold_from(1 - role, 1 - second, first)
    to_core[3].wait_recv()
    unfold_from(1 - role, 1 - second, 1 - first)
    table = token_ref[:, :, half:].astype(jnp.float32)[:, :tokens].reshape(total_rows, 128)
    mine = lax.broadcasted_iota(jnp.int32, (total_rows, 128), 1) == role * group_count + dev
    share = jnp.sum(jnp.where(mine, table, 0.0), axis=1, keepdims=True) / jnp.sum(
        table, axis=1, keepdims=True
    )

    span_width = half // pieces

    def sum_copy(source, target, device, number):
        return pltpu.make_async_remote_copy(
            src_ref=source,
            dst_ref=target,
            send_sem=sum_send.at[number],
            recv_sem=sum_recv.at[number],
            device_id=device,
            device_id_type=MESH,
        )

    core_sums = [
        sum_copy(part_ref.at[p, pl.ds((1 - role) * 16, 16)], core_in.at[p], other_core, 6 * p)
        for p in range(pieces)
    ]
    first_sums = [
        sum_copy(first_out.at[p], first_in.at[p], first_side, 6 * p + 1) for p in range(pieces)
    ]
    second_sums = [
        sum_copy(second_out.at[p], second_in.at[p], second_side, 6 * p + 2) for p in range(pieces)
    ]
    depth_sums = [
        [
            sum_copy(
                depth_out.at[p, k - 1],
                depth_in.at[p, k - 1],
                place_of(role, first, second, depths[k]),
                6 * p + 2 + k,
            )
            for k in (1, 2, 3)
        ]
        for p in range(pieces)
    ]

    left = low_ref[...].reshape(total_rows, half)
    right = high_ref[...].reshape(total_rows, half)

    def through(weight_ref):
        return jnp.dot(left, weight_ref[:half], preferred_element_type=jnp.float32) + jnp.dot(
            right, weight_ref[half:], preferred_element_type=jnp.float32
        )

    gate_part = through(gate_ref)
    up_part = through(up_ref)
    active_rows = (gate_part / (1.0 + jnp.exp(-gate_part)) * up_part).astype(jnp.bfloat16)

    def produce(p):
        sides = []
        for side in range(2):
            edge = side * half + p * span_width
            product = jnp.dot(
                active_rows, down_ref[:, edge : edge + span_width], preferred_element_type=jnp.float32
            )
            sides.append((product * share).reshape(2 * pairs, tokens, span_width))
        part_ref[p] = jnp.concatenate(sides, axis=1).astype(jnp.bfloat16)
        core_sums[p].start()

    def core_total(p, start, count):
        return part_ref[p, pl.ds(role * 16 + start, count)].astype(jnp.float32) + core_in[
            p, pl.ds(start, count)
        ].astype(jnp.float32)

    def pass_first(p):
        core_sums[p].wait_recv()
        first_out[p] = core_total(p, (1 - first) * 8, 8).astype(jnp.bfloat16)
        first_sums[p].start()

    def first_total(p, second_at, depth_at, count):
        start = second_at * 4 + depth_at
        return core_total(p, first * 8 + start, count) + first_in[p, pl.ds(start, count)].astype(
            jnp.float32
        )

    def pass_second(p):
        first_sums[p].wait_recv()
        second_out[p] = first_total(p, 1 - second, 0, 4).astype(jnp.bfloat16)
        second_sums[p].start()

    def second_total(p, depth_at):
        return first_total(p, second, depth_at, 1)[0] + second_in[p, depth_at].astype(jnp.float32)

    def pass_depth(p):
        second_sums[p].wait_recv()
        for k in (1, 2, 3):
            depth_out[p, k - 1] = second_total(p, depths[k]).astype(jnp.bfloat16)
            depth_sums[p][k - 1].start()

    def finish(p):
        total = second_total(p, depth)
        for k in range(3):
            depth_sums[p][k].wait_recv()
            total = total + depth_in[p, k].astype(jnp.float32)
        for side in range(2):
            edge = side * half + p * span_width
            span = slice(edge, edge + span_width)
            out_ref[:, span] = (
                residual_ref[:, span] + total[side * tokens : (side + 1) * tokens]
            )

    sent = to_depth + to_second + to_first + to_core

    def settle(p):
        share_of = -(-len(sent) // pieces)
        for copy in sent[p * share_of : (p + 1) * share_of]:
            copy.wait_send()
        for copy in (core_sums[p], first_sums[p], second_sums[p]):
            copy.wait_send()

    for p in range(pieces):
        produce(p)
        if p > 1:
            pass_first(p - 2)
    for p in range(max(pieces - 2, 0), pieces):
        pass_first(p)
    for p in range(pieces):
        pass_second(p)
        if p > 0:
            pass_depth(p - 1)
    pass_depth(pieces - 1)
    for p in range(pieces):
        settle(p)
    for p in range(pieces):
        finish(p)
    for group in depth_sums:
        for copy in group:
            copy.wait_send()


def fused_layer(
    queries,
    new_keys,
    new_values,
    lengths,
    cache_keys,
    cache_values,
    hidden,
    norm_gain,
    expert_ids,
    gate_levels,
    out_proj,
    gate_w,
    up_w,
    down_w,
):
    pieces = 4
    tokens, width = hidden.shape
    half = width // 2
    rows, heads, head_dim = queries.shape
    inner = heads * head_dim
    cached = cache_keys.shape[1] * cache_keys.shape[2]
    col_width = out_proj.shape[1]
    dev_count = lax.axis_size("dev")
    hidden_units = gate_w.shape[1]
    span = half // pieces
    bf16 = jnp.bfloat16
    vmem = pl.BlockSpec(memory_space=pltpu.VMEM)
    scalars = pl.BlockSpec(memory_space=pltpu.SMEM)
    anywhere = pl.BlockSpec(memory_space=pl.ANY)
    sems = pltpu.SemaphoreType.DMA
    out = pl.pallas_call(
        functools.partial(layer_kernel, pieces),
        out_shape=jax.ShapeDtypeStruct((tokens, width), jnp.float32),
        in_specs=[vmem] * 3 + [scalars] + [anywhere] * 2 + [vmem] * 4 + [anywhere] * 4,
        out_specs=vmem,
        scratch_shapes=[
            pltpu.VMEM((rows, cached, head_dim), bf16),
            pltpu.VMEM((rows, cached, head_dim), bf16),
            pltpu.VMEM((rows * heads, head_dim), jnp.float32),
            pltpu.VMEM((2, dev_count, rows, inner // 2), bf16),
            pltpu.VMEM((dev_count, rows, inner // 2), bf16),
            pltpu.VMEM((dev_count, rows, inner // 2), bf16),
            pltpu.VMEM(out_proj.shape, bf16),
            pltpu.VMEM((width, hidden_units), bf16),
            pltpu.VMEM((width, hidden_units), bf16),
            pltpu.VMEM((hidden_units, width), bf16),
            pltpu.VMEM((2 * dev_count, 2 * tokens, col_width // 2), bf16),
            pltpu.VMEM((2 * dev_count, 2 * tokens, col_width // 2), bf16),
            pltpu.VMEM((tokens, width), jnp.float32),
            pltpu.VMEM((4 * dev_count, 2 * tokens, half + 128), bf16),
            pltpu.VMEM((2 * dev_count, 2 * tokens, half), bf16),
            pltpu.VMEM((2 * dev_count, 2 * tokens, half), bf16),
            pltpu.VMEM((pieces, 32, 2 * tokens, span), bf16),
            pltpu.VMEM((pieces, 16, 2 * tokens, span), bf16),
            pltpu.VMEM((pieces, 8, 2 * tokens, span), bf16),
            pltpu.VMEM((pieces, 8, 2 * tokens, span), bf16),
            pltpu.VMEM((pieces, 4, 2 * tokens, span), bf16),
            pltpu.VMEM((pieces, 4, 2 * tokens, span), bf16),
            pltpu.VMEM((pieces, 3, 2 * tokens, span), bf16),
            pltpu.VMEM((pieces, 3, 2 * tokens, span), bf16),
            sems((6,)),
            sems((14,)),
            sems((14,)),
            sems((2 * dev_count - 1,)),
            sems((2 * dev_count - 1,)),
            sems((19,)),
            sems((19,)),
            sems((6 * pieces,)),
            sems((6 * pieces,)),
        ],
        compiler_params=pltpu.CompilerParams(
            collective_id=0, has_side_effects=True, vmem_limit_bytes=56 * 1024 * 1024
        ),
        cost_estimate=pl.CostEstimate(
            flops=3 * 2 * 256 * width * hidden_units, bytes_accessed=16 << 20, transcendentals=0
        ),
    )(
        queries,
        new_keys.reshape(2 * rows, head_dim),
        new_values.reshape(2 * rows, head_dim),
        lengths,
        cache_keys.reshape(rows, cached, head_dim),
        cache_values.reshape(rows, cached, head_dim),
        hidden,
        norm_gain.reshape(1, width),
        expert_ids,
        gate_levels,
        out_proj,
        gate_w,
        up_w,
        down_w,
    )
    return out.astype(bf16)


def on_device(
    hidden,
    queries,
    cache_keys,
    cache_values,
    new_keys,
    new_values,
    lengths,
    out_proj,
    norm_gain,
    expert_gate,
    expert_up,
    expert_down,
    expert_ids,
    gate_levels,
):
    sizes = tuple(lax.axis_size(name) for name in ("role", "dev", "head"))
    if sizes == (2, 8, 2) and hidden.shape[0] == 8 and queries.shape[0] == 16:
        return fused_layer(
            queries,
            new_keys,
            new_values,
            lengths,
            cache_keys,
            cache_values,
            hidden,
            norm_gain,
            expert_ids,
            gate_levels,
            out_proj,
            expert_gate[0],
            expert_up[0],
            expert_down[0],
        )
    attended = attend_block(queries, cache_keys, cache_values, new_keys, new_values, lengths)
    columns = jnp.dot(
        lax.all_gather(attended, "dev", axis=0, tiled=True),
        out_proj,
        preferred_element_type=jnp.float32,
    )
    dev_count = lax.axis_size("dev")
    head_count = lax.axis_size("head")
    experts = lax.axis_size("role") * dev_count
    col_width = out_proj.shape[1]
    width = dev_count * col_width
    projected = lax.all_to_all(columns, ("dev", "head"), split_axis=0, concat_axis=1, tiled=True)
    tokens = projected.shape[0]
    summed = jnp.sum(projected.reshape(tokens, dev_count, head_count, col_width), axis=2).reshape(
        tokens, width
    )
    residual = hidden.astype(jnp.float32) + summed
    normed = (
        residual
        * lax.rsqrt(jnp.mean(residual * residual, axis=-1, keepdims=True) + 1e-06)
        * norm_gain
    ).astype(jnp.bfloat16)
    top_k = expert_ids.shape[1]
    capacity = max(2, 2 * tokens * top_k // experts)
    own_ids = expert_ids.reshape(-1)
    own_ranks = slot_ranks(own_ids, experts)
    pair_rows, pair_ids = (
        lax.all_gather(normed, "head", axis=0, tiled=True),
        lax.all_gather(expert_ids, "head", axis=0, tiled=True),
    )
    pair_flat = pair_ids.reshape(head_count, tokens * top_k)
    pair_ranks = jax.vmap(lambda id_row: slot_ranks(id_row, experts))(pair_flat)
    pair_ranks = pair_ranks + capacity * jnp.arange(head_count, dtype=jnp.int32)[:, None]
    rows_from = jnp.arange(head_count * tokens * top_k, dtype=jnp.int32) // top_k
    outgoing = (
        jnp.zeros((experts, head_count * capacity, width), jnp.bfloat16)
        .at[pair_flat.reshape(-1), pair_ranks.reshape(-1)]
        .set(pair_rows[rows_from])
    )
    incoming = lax.all_to_all(outgoing, ("role", "dev"), split_axis=0, concat_axis=0, tiled=True)
    sources = incoming.shape[0]
    slot_total = incoming.shape[1]
    partial_value = expert_rows(
        incoming.reshape(sources * slot_total, width), expert_gate[0], expert_up[0], expert_down[0]
    )
    partial_value = partial_value.reshape(sources, slot_total, width).astype(jnp.bfloat16)
    arrived = lax.all_to_all(
        partial_value, ("role", "dev"), split_axis=0, concat_axis=0, tiled=True
    )
    arrived = (
        lax.psum_scatter(arrived, "head", scatter_dimension=1, tiled=True)
        .astype(jnp.float32)
        .astype(jnp.bfloat16)
    )
    picked = arrived[own_ids, own_ranks].astype(jnp.float32).reshape(tokens, top_k, width)
    levels = gate_levels.astype(jnp.float32)
    shares = levels / jnp.sum(levels, axis=1, keepdims=True)
    return (residual + jnp.sum(shares[..., None] * picked, axis=1)).astype(jnp.bfloat16)


def solution(mesh):
    placed = (
        P(("role", "dev", "head"), None),
        P(("role", "dev"), "head", None),
        P(("role", "dev"), None, "head", None),
        P(("role", "dev"), None, "head", None),
        P(("role", "dev"), "head", None),
        P(("role", "dev"), "head", None),
        P(("role", "dev")),
        P("head", "dev"),
        P(),
        P(("role", "dev"), None, "head"),
        P(("role", "dev"), None, "head"),
        P(("role", "dev"), "head", None),
        P(("role", "dev", "head"), None),
        P(("role", "dev", "head"), None),
    )
    return jax.shard_map(
        on_device,
        mesh=mesh,
        in_specs=placed,
        out_specs=P(("role", "dev", "head"), None),
        check_vma=False,
    )
```

```python
import functools
import math

import jax
import jax.numpy as jnp
from jax import lax
from jax.experimental import pallas as pl
from jax.experimental.pallas import tpu as pltpu
from jax.sharding import PartitionSpec as P

MESH = pl.DeviceIdType.MESH


def attend_block(query_rows, key_rows, value_rows, key_new, value_new, valid_len):
    row_count = query_rows.shape[0]
    kv_heads = key_rows.shape[2]
    group_size = query_rows.shape[1] // kv_heads
    head_dim = query_rows.shape[2]
    scaling = 1.0 / math.sqrt(head_dim)
    query_f = query_rows.astype(jnp.float32).reshape(row_count, kv_heads, group_size, head_dim)
    scores = jnp.einsum("bhgd,bthd->bhgt", query_f, key_rows.astype(jnp.float32)) * scaling
    scores_new = jnp.einsum("bhgd,bhd->bhg", query_f, key_new.astype(jnp.float32)) * scaling
    positions = jnp.arange(key_rows.shape[1], dtype=jnp.int32)
    usable = (positions[None, :] < valid_len[:, None])[:, None, None, :]
    masked = jnp.where(usable, scores, -1e30)
    highest = jnp.maximum(jnp.max(masked, axis=-1), scores_new)
    exp_terms = jnp.exp(masked - highest[..., None])
    exp_new = jnp.exp(scores_new - highest)
    totals = jnp.sum(exp_terms, axis=-1) + exp_new
    weights = (exp_terms / totals[..., None]).astype(jnp.bfloat16)
    weight_new = (exp_new / totals).astype(jnp.bfloat16)
    blended = jnp.einsum("bhgt,bthd->bhgd", weights, value_rows, preferred_element_type=jnp.float32)
    blended = (
        blended
        + weight_new.astype(jnp.float32)[..., None] * value_new.astype(jnp.float32)[:, :, None, :]
    )
    return blended.astype(jnp.bfloat16).reshape(row_count, kv_heads * group_size * head_dim)


def expert_rows(rows_in, gate_w, up_w, down_w):
    gate_part = jnp.dot(rows_in, gate_w, preferred_element_type=jnp.float32)
    up_part = jnp.dot(rows_in, up_w, preferred_element_type=jnp.float32)
    active = (jax.nn.silu(gate_part) * up_part).astype(jnp.bfloat16)
    return jnp.dot(active, down_w, preferred_element_type=jnp.float32)


def slot_ranks(flat_ids, experts):
    one_hot = (flat_ids[:, None] == jnp.arange(experts, dtype=jnp.int32)[None, :]).astype(jnp.int32)
    return jnp.sum(jnp.cumsum(one_hot, axis=0) * one_hot, axis=1) - 1


def place_of(role, first, second, depth):
    head = first * (1 - role) + second * role
    low = second * (1 - role) + first * role
    return (role, 2 * depth + low, head)


def partner_depths(depth):
    return (depth, depth + 1 - 2 * (depth % 2), depth + 2 - 4 * (depth // 2), 3 - depth)


def layer_kernel(
    pieces,
    query_ref,
    new_key_ref,
    new_value_ref,
    length_ref,
    keys_hbm,
    values_hbm,
    hidden_ref,
    gain_ref,
    ids_ref,
    levels_ref,
    proj_hbm,
    gate_hbm,
    up_hbm,
    down_hbm,
    out_ref,
    keys_ref,
    values_ref,
    att_ref,
    gathered,
    att_low,
    att_high,
    proj_ref,
    gate_ref,
    up_ref,
    down_ref,
    col_out,
    col_in,
    residual_ref,
    token_ref,
    low_ref,
    high_ref,
    active_ref,
    part_ref,
    core_in,
    first_out,
    first_in,
    second_out,
    second_in,
    depth_out,
    depth_in,
    weight_sems,
    att_send,
    att_recv,
    col_send,
    col_recv,
    tok_send,
    tok_recv,
    sum_send,
    sum_recv,
):
    role, dev, head = lax.axis_index("role"), lax.axis_index("dev"), lax.axis_index("head")
    group_count = gathered.shape[1]
    tokens = residual_ref.shape[0]
    width = residual_ref.shape[1]
    half = width // 2
    member = dev * 2 + head
    members = group_count * 2
    low, depth = dev % 2, dev // 2
    first = head * (1 - role) + low * role
    second = low * (1 - role) + head * role
    depths = partner_depths(depth)
    other_core = (1 - role, dev, head)

    loads = [
        pltpu.make_async_copy(source, target, weight_sems.at[number])
        for number, (source, target) in enumerate(
            (
                (proj_hbm, proj_ref),
                (gate_hbm, gate_ref),
                (up_hbm, up_ref),
                (down_hbm, down_ref),
                (keys_hbm, keys_ref),
                (values_hbm, values_ref),
            )
        )
    ]
    for load in loads[4:] + loads[:4]:
        load.start()

    barrier = pltpu.get_barrier_semaphore()

    def greet(step, carry):
        target = (member + step) % members
        pl.semaphore_signal(
            barrier, inc=1, device_id=(role, target // 2, target % 2), device_id_type=MESH
        )
        return carry

    lax.fori_loop(1, members, greet, 0)
    pl.semaphore_signal(barrier, inc=1, device_id=other_core, device_id_type=MESH)

    heads, head_dim = query_ref.shape[1:]
    slots = keys_ref.shape[1]
    shared = heads // 2
    scaling = 1.0 / math.sqrt(head_dim)
    column = lax.broadcasted_iota(jnp.int32, (heads, slots), 1)
    same_head = column % 2 == lax.broadcasted_iota(jnp.int32, (heads, slots), 0) // shared
    new_keys = new_key_ref[...].astype(jnp.float32)
    new_values = new_value_ref[...].astype(jnp.float32)

    def both_heads(rows, request):
        return jnp.concatenate(
            [
                jnp.broadcast_to(rows[2 * request + kv : 2 * request + kv + 1], (shared, head_dim))
                for kv in range(2)
            ],
            axis=0,
        )

    def attend(request):
        query = query_ref[request]
        scores = lax.dot_general(
            query,
            keys_ref[request],
            (((1,), (1,)), ((), ())),
            preferred_element_type=jnp.float32,
        )
        score_new = scaling * jnp.sum(
            query.astype(jnp.float32) * both_heads(new_keys, request), axis=1, keepdims=True
        )
        valid = same_head & (column < 2 * length_ref[:, request : request + 1])
        masked = jnp.where(valid, scores * scaling, -1e30)
        highest = jnp.maximum(jnp.max(masked, axis=1, keepdims=True), score_new)
        terms = jnp.exp(masked - highest)
        term_new = jnp.exp(score_new - highest)
        totals = jnp.sum(terms, axis=1, keepdims=True) + term_new
        weights = (terms / totals).astype(jnp.bfloat16)
        weight_new = (term_new / totals).astype(jnp.bfloat16).astype(jnp.float32)
        blended = jnp.dot(weights, values_ref[request], preferred_element_type=jnp.float32)
        att_ref[request * heads : (request + 1) * heads] = blended + weight_new * both_heads(
            new_values, request
        )

    def attend_half(part):
        for request in range(part * tokens, (part + 1) * tokens):
            attend(request)
        for j in range(shared):
            pair = [
                att_ref[pl.ds(part * tokens * heads + kv * shared + j, tokens, stride=heads), :]
                for kv in range(2)
            ]
            gathered[part, dev, :, j * head_dim : (j + 1) * head_dim] = jnp.concatenate(
                pair, axis=0
            ).astype(jnp.bfloat16)

    def att_copy(part, depth_from, target, number):
        block = gathered.at[part, 2 * depth_from + low]
        return pltpu.make_async_remote_copy(
            src_ref=block,
            dst_ref=block,
            send_sem=att_send.at[7 * part + number],
            recv_sem=att_recv.at[7 * part + number],
            device_id=target,
            device_id_type=MESH,
        )

    beside = (role, 2 * depth + 1 - low, head)
    along = [
        [att_copy(part, depth, (role, 2 * depths[k] + low, head), k - 1) for k in (1, 2, 3)]
        for part in range(2)
    ]
    across = [
        [att_copy(part, depths[k], beside, 3 + k) for k in range(4)] for part in range(2)
    ]
    loads[4].wait()
    loads[5].wait()
    for part in range(2):
        attend_half(part)
        if part == 0:
            pl.semaphore_wait(barrier, members)
        across[part][0].start()
        for copy in along[part]:
            copy.start()

    def unfold_att(block):
        one = gathered[0, block].astype(jnp.float32)
        two = gathered[1, block].astype(jnp.float32)
        att_low[block] = jnp.concatenate([one[:tokens], two[:tokens]], axis=0).astype(jnp.bfloat16)
        att_high[block] = jnp.concatenate([one[tokens:], two[tokens:]], axis=0).astype(
            jnp.bfloat16
        )

    for part in range(2):
        for k in (1, 2, 3):
            along[part][k - 1].wait_recv()
            across[part][k].start()
    for k in range(4):
        unfold_att(2 * depths[k] + low)
    for k in range(4):
        across[0][k].wait_recv()
    for k in range(4):
        across[1][k].wait_recv()
        unfold_att(2 * depths[k] + 1 - low)

    loads[0].wait()
    fold = att_low.shape[2]
    rows = group_count * 2 * tokens
    columns = jnp.dot(
        att_low[...].reshape(rows, fold), proj_ref[:fold], preferred_element_type=jnp.float32
    ) + jnp.dot(
        att_high[...].reshape(rows, fold), proj_ref[fold:], preferred_element_type=jnp.float32
    )
    col_width = columns.shape[1]
    columns = columns.reshape(members, tokens, col_width)
    col_out[...] = jnp.concatenate(
        [columns[:, :, : col_width // 2], columns[:, :, col_width // 2 :]], axis=1
    ).astype(jnp.bfloat16)

    def col_copy(step):
        target = (member + step) % members
        return pltpu.make_async_remote_copy(
            src_ref=col_out.at[target],
            dst_ref=col_in.at[member],
            send_sem=col_send.at[step - 1],
            recv_sem=col_recv.at[step - 1],
            device_id=(role, target // 2, target % 2),
            device_id_type=MESH,
        )

    def col_start(step, carry):
        col_copy(step).start()
        return carry

    def col_sent(step, carry):
        col_copy(step).wait_send()
        return carry

    def col_arrive(step, carry):
        col_copy(step).wait_recv()
        return carry

    lax.fori_loop(1, members, col_start, 0)
    col_in[member] = col_out[member]
    lanes = lax.broadcasted_iota(jnp.int32, (tokens, 128), 1)
    named = jnp.zeros((tokens, 128), jnp.float32)
    for k in range(ids_ref.shape[1]):
        level = levels_ref[:, k : k + 1].astype(jnp.float32)
        named = named + jnp.where(lanes == ids_ref[:, k : k + 1], level, 0.0)
    slot = role * 16 + first * 8 + second * 4 + depth
    token_ref[slot, :, half:] = jnp.concatenate(
        [named, jnp.zeros((tokens, 128), jnp.float32)], axis=0
    ).astype(jnp.bfloat16)
    lax.fori_loop(1, members, col_arrive, 0)

    for block in range(group_count):
        both = col_in[2 * block].astype(jnp.float32) + col_in[2 * block + 1].astype(jnp.float32)
        for side in range(2):
            edge = block * col_width + side * (col_width // 2)
            span = slice(edge, edge + col_width // 2)
            residual_ref[:, span] = (
                hidden_ref[:, span].astype(jnp.float32) + both[side * tokens : (side + 1) * tokens]
            )
    residual = residual_ref[...]
    square = jnp.sum(residual * residual, axis=-1, keepdims=True) / width
    normed = residual * lax.rsqrt(square + 1e-06) * gain_ref[...]
    token_ref[slot, :, :half] = jnp.concatenate(
        [normed[:, :half], normed[:, half:]], axis=0
    ).astype(jnp.bfloat16)

    def token_copy(start, count, target, number):
        block = token_ref.at[pl.ds(start, count)]
        return pltpu.make_async_remote_copy(
            src_ref=block,
            dst_ref=block,
            send_sem=tok_send.at[number],
            recv_sem=tok_recv.at[number],
            device_id=target,
            device_id_type=MESH,
        )

    def slot_of(first_at, second_at, depth_at):
        return role * 16 + first_at * 8 + second_at * 4 + depth_at

    second_side = place_of(role, first, 1 - second, depth)
    first_side = place_of(role, 1 - first, second, depth)
    own = [slot_of(first, second, depths[k]) for k in range(4)]
    near = [slot_of(first, 1 - second, depths[k]) for k in range(4)]
    to_depth = [
        token_copy(own[0], 1, place_of(role, first, second, depths[k]), k - 1) for k in (1, 2, 3)
    ]
    to_second = [token_copy(own[k], 1, second_side, 3 + k) for k in range(4)]
    to_first = [token_copy(own[k], 1, first_side, 7 + k) for k in range(4)]
    to_first = to_first + [token_copy(near[k], 1, first_side, 11 + k) for k in range(4)]
    to_core = [
        token_copy(slot_of(*corner, 0), 4, other_core, 15 + number)
        for number, corner in enumerate(
            ((first, second), (first, 1 - second), (1 - first, second), (1 - first, 1 - second))
        )
    ]
    to_second[0].start()
    to_first[0].start()
    for copy in to_depth:
        copy.start()
    for k in (1, 2, 3):
        to_depth[k - 1].wait_recv()
        to_second[k].start()
        to_first[k].start()
    to_core[0].start()

    def unfold(pair, carry):
        one = token_ref[2 * pair, :, :half].astype(jnp.float32)
        two = token_ref[2 * pair + 1, :, :half].astype(jnp.float32)
        low_ref[pair] = jnp.concatenate([one[:tokens], two[:tokens]], axis=0).astype(jnp.bfloat16)
        high_ref[pair] = jnp.concatenate([one[tokens:], two[tokens:]], axis=0).astype(jnp.bfloat16)
        return carry

    def unfold_from(role_at, first_at, second_at):
        start = role_at * 8 + first_at * 4 + second_at * 2
        lax.fori_loop(start, start + 2, unfold, 0)

    pairs = low_ref.shape[0]
    total_rows = pairs * 2 * tokens
    set_rows = total_rows // 4
    set_pairs = pairs // 4

    def expert_set(first_own, first_other):
        sides = []
        for ref in (low_ref, high_ref):
            both = [
                ref[pl.ds(role * 8 + first_own * 4, set_pairs)],
                ref[pl.ds((1 - role) * 8 + first_other * 4, set_pairs)],
            ]
            sides.append(jnp.concatenate(both, axis=0).reshape(2 * set_rows, half))

        def through(weight_ref):
            return jnp.dot(
                sides[0], weight_ref[:half], preferred_element_type=jnp.float32
            ) + jnp.dot(sides[1], weight_ref[half:], preferred_element_type=jnp.float32)

        gate_part = through(gate_ref)
        up_part = through(up_ref)
        active = (gate_part / (1.0 + jnp.exp(-gate_part)) * up_part).astype(jnp.bfloat16)
        active_ref[role * 2 + first_own] = active[:set_rows]
        active_ref[(1 - role) * 2 + first_other] = active[set_rows:]

    unfold_from(role, first, second)
    for k in range(4):
        to_second[k].wait_recv()
        to_first[4 + k].start()
    to_core[1].start()
    unfold_from(role, first, 1 - second)
    lax.fori_loop(1, members, col_sent, 0)
    for part in range(2):
        for copy in along[part] + across[part]:
            copy.wait_send()
    for load in loads[1:4]:
        load.wait()
    for k in range(4):
        to_first[k].wait_recv()
    to_core[2].start()
    unfold_from(role, 1 - first, second)
    to_core[0].wait_recv()
    unfold_from(1 - role, second, first)
    to_core[1].wait_recv()
    unfold_from(1 - role, second, 1 - first)
    expert_set(first, second)
    for k in range(4, 8):
        to_first[k].wait_recv()
    to_core[3].start()
    unfold_from(role, 1 - first, 1 - second)
    to_core[2].wait_recv()
    unfold_from(1 - role, 1 - second, first)
    to_core[3].wait_recv()
    unfold_from(1 - role, 1 - second, 1 - first)
    expert_set(1 - first, 1 - second)
    table = token_ref[:, :, half:].astype(jnp.float32)[:, :tokens].reshape(total_rows, 128)
    mine = lax.broadcasted_iota(jnp.int32, (total_rows, 128), 1) == role * group_count + dev
    share = jnp.sum(jnp.where(mine, table, 0.0), axis=1, keepdims=True) / jnp.sum(
        table, axis=1, keepdims=True
    )

    span_width = half // pieces

    def sum_copy(source, target, device, number):
        return pltpu.make_async_remote_copy(
            src_ref=source,
            dst_ref=target,
            send_sem=sum_send.at[number],
            recv_sem=sum_recv.at[number],
            device_id=device,
            device_id_type=MESH,
        )

    core_sums = [
        sum_copy(part_ref.at[p, pl.ds((1 - role) * 16, 16)], core_in.at[p], other_core, 6 * p)
        for p in range(pieces)
    ]
    first_sums = [
        sum_copy(first_out.at[p], first_in.at[p], first_side, 6 * p + 1) for p in range(pieces)
    ]
    second_sums = [
        sum_copy(second_out.at[p], second_in.at[p], second_side, 6 * p + 2) for p in range(pieces)
    ]
    depth_sums = [
        [
            sum_copy(
                depth_out.at[p, k - 1],
                depth_in.at[p, k - 1],
                place_of(role, first, second, depths[k]),
                6 * p + 2 + k,
            )
            for k in (1, 2, 3)
        ]
        for p in range(pieces)
    ]

    active_rows = active_ref[...].reshape(total_rows, active_ref.shape[2])

    def produce(p):
        sides = []
        for side in range(2):
            edge = side * half + p * span_width
            product = jnp.dot(
                active_rows, down_ref[:, edge : edge + span_width], preferred_element_type=jnp.float32
            )
            sides.append((product * share).reshape(2 * pairs, tokens, span_width))
        part_ref[p] = jnp.concatenate(sides, axis=1).astype(jnp.bfloat16)
        core_sums[p].start()

    def core_total(p, start, count):
        return part_ref[p, pl.ds(role * 16 + start, count)].astype(jnp.float32) + core_in[
            p, pl.ds(start, count)
        ].astype(jnp.float32)

    def pass_first(p):
        core_sums[p].wait_recv()
        first_out[p] = core_total(p, (1 - first) * 8, 8).astype(jnp.bfloat16)
        first_sums[p].start()

    def first_total(p, second_at, depth_at, count):
        start = second_at * 4 + depth_at
        return core_total(p, first * 8 + start, count) + first_in[p, pl.ds(start, count)].astype(
            jnp.float32
        )

    def pass_second(p):
        first_sums[p].wait_recv()
        second_out[p] = first_total(p, 1 - second, 0, 4).astype(jnp.bfloat16)
        second_sums[p].start()

    def second_total(p, depth_at):
        return first_total(p, second, depth_at, 1)[0] + second_in[p, depth_at].astype(jnp.float32)

    def pass_depth(p):
        second_sums[p].wait_recv()
        for k in (1, 2, 3):
            depth_out[p, k - 1] = second_total(p, depths[k]).astype(jnp.bfloat16)
            depth_sums[p][k - 1].start()

    def finish(p):
        total = second_total(p, depth)
        for k in range(3):
            depth_sums[p][k].wait_recv()
            total = total + depth_in[p, k].astype(jnp.float32)
        for side in range(2):
            edge = side * half + p * span_width
            span = slice(edge, edge + span_width)
            out_ref[:, span] = (
                residual_ref[:, span] + total[side * tokens : (side + 1) * tokens]
            )

    sent = to_depth + to_second + to_first + to_core

    def settle(p):
        share_of = -(-len(sent) // pieces)
        for copy in sent[p * share_of : (p + 1) * share_of]:
            copy.wait_send()
        for copy in (core_sums[p], first_sums[p], second_sums[p]):
            copy.wait_send()

    steps = ((produce, 0), (pass_first, 1), (pass_second, 2), (pass_depth, 3), (finish, 5))
    for turn in range(pieces + 5):
        for step, lag in steps:
            if 0 <= turn - lag < pieces:
                step(turn - lag)
                if step is pass_depth:
                    settle(turn - lag)

    for group in depth_sums:
        for copy in group:
            copy.wait_send()


def fused_layer(
    queries,
    new_keys,
    new_values,
    lengths,
    cache_keys,
    cache_values,
    hidden,
    norm_gain,
    expert_ids,
    gate_levels,
    out_proj,
    gate_w,
    up_w,
    down_w,
):
    pieces = 4
    tokens, width = hidden.shape
    half = width // 2
    rows, heads, head_dim = queries.shape
    inner = heads * head_dim
    cached = cache_keys.shape[1] * cache_keys.shape[2]
    col_width = out_proj.shape[1]
    dev_count = lax.axis_size("dev")
    hidden_units = gate_w.shape[1]
    span = half // pieces
    bf16 = jnp.bfloat16
    vmem = pl.BlockSpec(memory_space=pltpu.VMEM)
    anywhere = pl.BlockSpec(memory_space=pl.ANY)
    sems = pltpu.SemaphoreType.DMA
    out = pl.pallas_call(
        functools.partial(layer_kernel, pieces),
        out_shape=jax.ShapeDtypeStruct((tokens, width), jnp.float32),
        in_specs=[vmem] * 4 + [anywhere] * 2 + [vmem] * 4 + [anywhere] * 4,
        out_specs=vmem,
        scratch_shapes=[
            pltpu.VMEM((rows, cached, head_dim), bf16),
            pltpu.VMEM((rows, cached, head_dim), bf16),
            pltpu.VMEM((rows * heads, head_dim), jnp.float32),
            pltpu.VMEM((2, dev_count, rows, inner // 2), bf16),
            pltpu.VMEM((dev_count, rows, inner // 2), bf16),
            pltpu.VMEM((dev_count, rows, inner // 2), bf16),
            pltpu.VMEM(out_proj.shape, bf16),
            pltpu.VMEM((width, hidden_units), bf16),
            pltpu.VMEM((width, hidden_units), bf16),
            pltpu.VMEM((hidden_units, width), bf16),
            pltpu.VMEM((2 * dev_count, 2 * tokens, col_width // 2), bf16),
            pltpu.VMEM((2 * dev_count, 2 * tokens, col_width // 2), bf16),
            pltpu.VMEM((tokens, width), jnp.float32),
            pltpu.VMEM((4 * dev_count, 2 * tokens, half + 128), bf16),
            pltpu.VMEM((2 * dev_count, 2 * tokens, half), bf16),
            pltpu.VMEM((2 * dev_count, 2 * tokens, half), bf16),
            pltpu.VMEM((4, 8 * tokens, hidden_units), bf16),
            pltpu.VMEM((pieces, 32, 2 * tokens, span), bf16),
            pltpu.VMEM((pieces, 16, 2 * tokens, span), bf16),
            pltpu.VMEM((pieces, 8, 2 * tokens, span), bf16),
            pltpu.VMEM((pieces, 8, 2 * tokens, span), bf16),
            pltpu.VMEM((pieces, 4, 2 * tokens, span), bf16),
            pltpu.VMEM((pieces, 4, 2 * tokens, span), bf16),
            pltpu.VMEM((pieces, 3, 2 * tokens, span), bf16),
            pltpu.VMEM((pieces, 3, 2 * tokens, span), bf16),
            sems((6,)),
            sems((14,)),
            sems((14,)),
            sems((2 * dev_count - 1,)),
            sems((2 * dev_count - 1,)),
            sems((19,)),
            sems((19,)),
            sems((6 * pieces,)),
            sems((6 * pieces,)),
        ],
        compiler_params=pltpu.CompilerParams(
            collective_id=0, has_side_effects=True, vmem_limit_bytes=56 * 1024 * 1024
        ),
        cost_estimate=pl.CostEstimate(
            flops=3 * 2 * 256 * width * hidden_units, bytes_accessed=16 << 20, transcendentals=0
        ),
    )(
        queries,
        new_keys.reshape(2 * rows, head_dim),
        new_values.reshape(2 * rows, head_dim),
        lengths.reshape(1, rows),
        cache_keys.reshape(rows, cached, head_dim),
        cache_values.reshape(rows, cached, head_dim),
        hidden,
        norm_gain.reshape(1, width),
        expert_ids,
        gate_levels,
        out_proj,
        gate_w,
        up_w,
        down_w,
    )
    return out.astype(bf16)


def on_device(
    hidden,
    queries,
    cache_keys,
    cache_values,
    new_keys,
    new_values,
    lengths,
    out_proj,
    norm_gain,
    expert_gate,
    expert_up,
    expert_down,
    expert_ids,
    gate_levels,
):
    sizes = tuple(lax.axis_size(name) for name in ("role", "dev", "head"))
    if sizes == (2, 8, 2) and hidden.shape[0] == 8 and queries.shape[0] == 16:
        return fused_layer(
            queries,
            new_keys,
            new_values,
            lengths,
            cache_keys,
            cache_values,
            hidden,
            norm_gain,
            expert_ids,
            gate_levels,
            out_proj,
            expert_gate[0],
            expert_up[0],
            expert_down[0],
        )
    attended = attend_block(queries, cache_keys, cache_values, new_keys, new_values, lengths)
    columns = jnp.dot(
        lax.all_gather(attended, "dev", axis=0, tiled=True),
        out_proj,
        preferred_element_type=jnp.float32,
    )
    dev_count = lax.axis_size("dev")
    head_count = lax.axis_size("head")
    experts = lax.axis_size("role") * dev_count
    col_width = out_proj.shape[1]
    width = dev_count * col_width
    projected = lax.all_to_all(columns, ("dev", "head"), split_axis=0, concat_axis=1, tiled=True)
    tokens = projected.shape[0]
    summed = jnp.sum(projected.reshape(tokens, dev_count, head_count, col_width), axis=2).reshape(
        tokens, width
    )
    residual = hidden.astype(jnp.float32) + summed
    normed = (
        residual
        * lax.rsqrt(jnp.mean(residual * residual, axis=-1, keepdims=True) + 1e-06)
        * norm_gain
    ).astype(jnp.bfloat16)
    top_k = expert_ids.shape[1]
    capacity = max(2, 2 * tokens * top_k // experts)
    own_ids = expert_ids.reshape(-1)
    own_ranks = slot_ranks(own_ids, experts)
    pair_rows, pair_ids = (
        lax.all_gather(normed, "head", axis=0, tiled=True),
        lax.all_gather(expert_ids, "head", axis=0, tiled=True),
    )
    pair_flat = pair_ids.reshape(head_count, tokens * top_k)
    pair_ranks = jax.vmap(lambda id_row: slot_ranks(id_row, experts))(pair_flat)
    pair_ranks = pair_ranks + capacity * jnp.arange(head_count, dtype=jnp.int32)[:, None]
    rows_from = jnp.arange(head_count * tokens * top_k, dtype=jnp.int32) // top_k
    outgoing = (
        jnp.zeros((experts, head_count * capacity, width), jnp.bfloat16)
        .at[pair_flat.reshape(-1), pair_ranks.reshape(-1)]
        .set(pair_rows[rows_from])
    )
    incoming = lax.all_to_all(outgoing, ("role", "dev"), split_axis=0, concat_axis=0, tiled=True)
    sources = incoming.shape[0]
    slot_total = incoming.shape[1]
    partial_value = expert_rows(
        incoming.reshape(sources * slot_total, width), expert_gate[0], expert_up[0], expert_down[0]
    )
    partial_value = partial_value.reshape(sources, slot_total, width).astype(jnp.bfloat16)
    arrived = lax.all_to_all(
        partial_value, ("role", "dev"), split_axis=0, concat_axis=0, tiled=True
    )
    arrived = (
        lax.psum_scatter(arrived, "head", scatter_dimension=1, tiled=True)
        .astype(jnp.float32)
        .astype(jnp.bfloat16)
    )
    picked = arrived[own_ids, own_ranks].astype(jnp.float32).reshape(tokens, top_k, width)
    levels = gate_levels.astype(jnp.float32)
    shares = levels / jnp.sum(levels, axis=1, keepdims=True)
    return (residual + jnp.sum(shares[..., None] * picked, axis=1)).astype(jnp.bfloat16)


def solution(mesh):
    placed = (
        P(("role", "dev", "head"), None),
        P(("role", "dev"), "head", None),
        P(("role", "dev"), None, "head", None),
        P(("role", "dev"), None, "head", None),
        P(("role", "dev"), "head", None),
        P(("role", "dev"), "head", None),
        P(("role", "dev")),
        P("head", "dev"),
        P(),
        P(("role", "dev"), None, "head"),
        P(("role", "dev"), None, "head"),
        P(("role", "dev"), "head", None),
        P(("role", "dev", "head"), None),
        P(("role", "dev", "head"), None),
    )
    return jax.shard_map(
        on_device,
        mesh=mesh,
        in_specs=placed,
        out_specs=P(("role", "dev", "head"), None),
        check_vma=False,
    )
```
